512 devices in a mesh: dp: 128 (over z, x, core), grp: 4 (over y).
Axes of the slice: x: 4, y: 4, z: 16, core: 2. Of those that a mesh axis runs over, the one named last changes fastest.
Arguments:
- queries: bfloat16 [32768, 4096], P('dp', 'grp'), may hold values from -6 to 6
- passages: bfloat16 [256, 128, 4096], P(None, 'dp', 'grp'), may hold values from -6 to 6
- block_lists: int32 [256, 3], P('dp'), may hold values from 0 to 255
- list_lengths: int32 [256], P('dp'), may hold values from 1 to 3, as said below
- positive: int32 [32768], P('dp'), may hold values from 0 to 32767, as said below
- loss_grad: float32 [32768], P('dp'), may hold values from -16 to 16
Outputs:
- losses: float32 [32768], P('dp')
- grad_queries: bfloat16 [32768, 4096], P('dp', 'grp')
- grad_passages: bfloat16 [256, 128, 4096], P(None, 'dp', 'grp')
The draws below stay inside these ranges and needn't reach their ends.
Inputs may be any that keep to these rules, and one draw needn't show every extreme that they name: `block_lists`: entries of a list past its length are ignored. `list_lengths`: the 2 query blocks of one dp index list 4 blocks or fewer together; in every draw some dp index lists exactly 4, with one of its blocks listing 3. positive[q] = n * 128 + r with r == q // 256.
All inputs are finite; a program needn't handle non-finite values.
Results may differ from the reference program's by a relative error of at most 0.0052.
Values may be sent and summed in bfloat16 or wider, within the bound.
A program may use at most 64 MiB of HBM per device.

```python
import math
import jax
import jax.numpy as jnp
from jax import lax

D = 4096
BLOCK = 128
LIST_MAX = 3
QB_DEV = 2
NQB = 256
NQ = 32768
NPB = 256
LIVE_MAX = 4
N_DP = 128


def draw_queries(key, part):
    noise = jax.random.normal(jax.random.fold_in(key, 1), (NQ, D), jnp.float32)
    values = noise
    return jnp.clip(values, -6.0, 6.0).astype(jnp.bfloat16)


def draw_passages(key, part):
    noise = jax.random.normal(jax.random.fold_in(key, 5), (NPB, BLOCK, D), jnp.float32)
    values = noise
    return jnp.clip(values, -6.0, 6.0).astype(jnp.bfloat16)


def draw_list_lengths(key, part):
    owners = NQB // QB_DEV
    budget = LIVE_MAX - QB_DEV
    extra_raw = jax.random.randint(jax.random.fold_in(key, 1), (owners, QB_DEV), 0, LIST_MAX)
    running = jnp.cumsum(extra_raw, axis=1) - extra_raw
    room = jnp.maximum(budget - running, 0)
    extras = jnp.minimum(extra_raw, room)
    heavy = jax.random.randint(jax.random.fold_in(key, 2), (), 0, owners)
    ranking = jax.random.permutation(jax.random.fold_in(key, 3), QB_DEV).astype(jnp.int32)
    heavy_extras = jnp.clip(budget - (LIST_MAX - 1) * ranking, 0, LIST_MAX - 1)
    owner_index = jnp.arange(owners, dtype=jnp.int32)[:, None]
    extras = jnp.where(owner_index == heavy, heavy_extras[None, :], extras)
    return (1 + extras).reshape(NQB).astype(jnp.int32)


def draw_positive(key, part):
    owners = NQB // QB_DEV
    shard_rows = BLOCK // owners
    query_owner = jnp.arange(NQ, dtype=jnp.int32) // (QB_DEV * BLOCK)
    block_pick = jax.random.randint(jax.random.fold_in(key, 1), (NQ,), 0, NPB)
    row_pick = jax.random.randint(jax.random.fold_in(key, 2), (NQ,), 0, shard_rows)
    return (block_pick * BLOCK + query_owner * shard_rows + row_pick).astype(jnp.int32)


def plant(array, own_key, smallest, high):
    longest = array.shape.index(max(array.shape))
    spots = []
    for shift in (0, 1):
        where = [jax.random.randint(jax.random.fold_in(own_key, axis), (), 0, length) for axis, length in enumerate(array.shape)]
        where[longest] = (where[longest] + shift) % array.shape[longest]
        spots.append(tuple(where))
    return array.at[spots[0]].set(smallest).at[spots[1]].set(high)


def steps_of(rng, extent, pieces, smallest, largest):
    def one(dim, blocks):
        heights = jax.random.uniform(jax.random.fold_in(jax.random.fold_in(rng, 6), dim), (blocks,), jnp.float32, smallest / len(pieces), largest / len(pieces))
        return jnp.repeat(jnp.exp(heights), extent[dim] // blocks).reshape((-1,) + (1,) * (len(extent) - dim - 1))

    loudness = one(*pieces[0])
    for cut in pieces[1:]:
        loudness = loudness * one(*cut)
    return loudness


def scatter_about(stream_key, shape, scale, reach, cuts=(), held_as=jnp.bfloat16):
    level = steps_of(stream_key, shape, cuts, -0.22, 0.18) if cuts else 1.0
    result = jax.random.normal(stream_key, shape, jnp.float32) * scale * level
    return jnp.minimum(jnp.maximum(result, -reach), reach).astype(held_as)


def setup_inputs(seed: int = 0) -> dict:
    key_list = jax.random.split(jax.random.key(seed), 7)
    return {
        "queries": draw_queries(jax.random.fold_in(key_list[6], 71), 0),
        "passages": draw_passages(jax.random.fold_in(key_list[6], 71), 0),
        "block_lists": plant(jax.random.randint(key_list[2], (NQB, LIST_MAX), 0, NPB), jax.random.fold_in(key_list[2], 1), 0, NPB - 1).astype(jnp.int32),
        "list_lengths": draw_list_lengths(jax.random.fold_in(key_list[6], 71), 0),
        "positive": draw_positive(jax.random.fold_in(key_list[6], 71), 0),
        "loss_grad": scatter_about(key_list[5], (NQ,), 4.0, 16.0, ((0, 128),), jnp.float32),
    }


def reference(queries, passages, block_lists, list_lengths, positive, loss_grad):
    score_scale = 3.0 / math.sqrt(D)
    shard_rows = BLOCK // N_DP
    query_rows = QB_DEV * BLOCK
    block_total = passages.shape[0]
    entry_index = jnp.arange(LIST_MAX, dtype=jnp.int32)
    column_index = jnp.arange(block_total * shard_rows, dtype=jnp.int32)

    def owner_step(carry, dp_owner):
        first = dp_owner * query_rows
        own_queries = lax.dynamic_slice_in_dim(queries, first, query_rows, 0)
        own_positive = lax.dynamic_slice_in_dim(positive, first, query_rows, 0)
        own_grad = lax.dynamic_slice_in_dim(loss_grad, first, query_rows, 0)
        own_lists = lax.dynamic_slice_in_dim(block_lists, dp_owner * QB_DEV, QB_DEV, 0)
        own_lengths = lax.dynamic_slice_in_dim(list_lengths, dp_owner * QB_DEV, QB_DEV, 0)
        row_start = dp_owner * shard_rows
        in_batch = lax.dynamic_slice_in_dim(passages, row_start, shard_rows, 1)
        in_flat = in_batch.reshape(block_total * shard_rows, D)
        scores_in = score_scale * jnp.dot(own_queries, in_flat.T, preferred_element_type=jnp.float32)
        listed = passages[own_lists.reshape(-1)].reshape(QB_DEV, LIST_MAX, BLOCK, D).astype(jnp.float32)
        query_blocks = own_queries.reshape(QB_DEV, BLOCK, D).astype(jnp.float32)
        scores_list = score_scale * jnp.einsum('bqf,blpf->bqlp', query_blocks, listed)
        slot_live = (entry_index[None, :] < own_lengths[:, None])[:, None, :, None]
        list_peak = lax.optimization_barrier(jnp.max(jnp.where(slot_live, scores_list, -jnp.inf), axis=(2, 3))).reshape(query_rows)
        row_peak = jnp.maximum(lax.optimization_barrier(jnp.max(scores_in, axis=1)), list_peak)
        peak_blocks = row_peak.reshape(QB_DEV, BLOCK, 1, 1)
        list_total = lax.optimization_barrier(jnp.sum(jnp.where(slot_live, jnp.exp(scores_list - peak_blocks), 0.0), axis=(2, 3))).reshape(query_rows)
        row_total = lax.optimization_barrier(jnp.sum(jnp.exp(scores_in - row_peak[:, None]), axis=1)) + list_total
        log_total = row_peak + jnp.log(row_total)
        pos_column = own_positive // BLOCK * shard_rows + own_positive % BLOCK - row_start
        is_positive = column_index[None, :] == pos_column[:, None]
        positive_score = lax.optimization_barrier(jnp.sum(jnp.where(is_positive, scores_in, 0.0), axis=1))
        losses = log_total - positive_score
        weights_in = (own_grad[:, None] * (jnp.exp(scores_in - log_total[:, None]) - is_positive.astype(jnp.float32))).astype(jnp.bfloat16)
        log_blocks = log_total.reshape(QB_DEV, BLOCK, 1, 1)
        grad_blocks = own_grad.reshape(QB_DEV, BLOCK, 1, 1)
        weights_list = jnp.where(slot_live, grad_blocks * jnp.exp(scores_list - log_blocks), 0.0).astype(jnp.bfloat16)
        near_terms = jnp.dot(weights_in, in_flat, preferred_element_type=jnp.float32)
        far_terms = jnp.einsum('bqlp,blpf->bqf', weights_list.astype(jnp.float32), listed).reshape(query_rows, D)
        grad_queries = (score_scale * (near_terms + far_terms)).astype(jnp.bfloat16)
        own_part = score_scale * jnp.dot(weights_in.T, own_queries, preferred_element_type=jnp.float32)
        shares = (score_scale * jnp.einsum('bqlp,bqf->blpf', weights_list.astype(jnp.float32), query_blocks)).astype(jnp.bfloat16)
        current = lax.dynamic_slice_in_dim(carry, row_start, shard_rows, 1)
        carry = lax.dynamic_update_slice_in_dim(carry, current + own_part.reshape(block_total, shard_rows, D), row_start, 1)
        carry = carry.at[own_lists.reshape(-1)].add(shares.reshape(QB_DEV * LIST_MAX, BLOCK, D).astype(jnp.float32))
        return (carry, (losses, grad_queries))
    start = jnp.zeros((block_total, BLOCK, D), jnp.float32)
    summed, outputs = lax.scan(owner_step, start, jnp.arange(N_DP, dtype=jnp.int32))
    losses, grad_queries = outputs
    return (losses.reshape(-1), grad_queries.reshape(-1, D), summed.astype(jnp.bfloat16))
```

```python
import functools
import math

import jax
import jax.numpy as jnp
from jax import lax
from jax.experimental import pallas as pl
from jax.experimental.pallas import tpu as pltpu
from jax.sharding import PartitionSpec as P

D = 4096
SCALE = 3.0 / math.sqrt(D)
SLOTS = 4
LOGICAL = pl.DeviceIdType.LOGICAL
NN = (((1,), (0,)), ((), ()))
NT = (((1,), (1,)), ((), ()))
F32, BF16 = jnp.float32, jnp.bfloat16


def mm(a, b, dims=NN):
    return lax.dot_general(a, b, dims, preferred_element_type=F32)


def kernel(
    z_count,
    q_ref, p_ref, lists_ref, lens_ref, pos_ref, lg_ref,
    loss_ref, gq_ref, gp_ref,
    ids, send1, recv1, send2, recv2, wide, listed, hot_t,
    part_in, recv_in, part_l, recv_l, sum_in, cols,
    wl_all, wi_all, ls_all, w_in, w_full, w_full_t, own,
    ids_s, ids_r, e1_s, e1_r, e2_s, e2_r, ri_s, ri_r, rl_s, rl_r, al_s, al_r, ai_s, ai_r, ls_s, ls_r, loc,
):
    me = lax.axis_index("dp")
    y = lax.axis_index("grp")
    n_dp = lax.axis_size("dp")
    n_y = lax.axis_size("grp")
    plane = n_dp // z_count
    my_z, my_xc = me // plane, me % plane
    block = q_ref.shape[0] // 2
    rows = block // n_y
    chunks = q_ref.shape[1] // 128
    msg = SLOTS * chunks

    def device(p, g):
        return p * n_y + g

    def copy_to(src, dst, ss, rs, dev):
        return pltpu.make_async_remote_copy(
            src_ref=src, dst_ref=dst, send_sem=ss, recv_sem=rs, device_id=dev, device_id_type=LOGICAL
        )

    def wait_bytes(ref, sem):
        pltpu.make_async_copy(ref, ref, sem).wait()

    def each_peer(body):
        def step(p, carry):
            body(p)
            return carry

        lax.fori_loop(me + 1, n_dp, step, 0)
        lax.fori_loop(0, me, step, 0)

    def far_first(body):
        def step(i, carry):
            j = z_count - 1 - i // plane
            k = plane - 1 - i % plane
            half = (j + 1) // 2
            dz = jnp.where(j % 2 == 1, half, z_count - half)
            body((my_z + dz) % z_count * plane + (my_xc + k) % plane)
            return carry

        lax.fori_loop(0, n_dp - 1, step, 0)

    barrier = pltpu.get_barrier_semaphore()
    each_peer(
        lambda p: pl.semaphore_signal(barrier, inc=1, device_id=device(p, y), device_id_type=LOGICAL)
    )
    for k in range(1, n_y):
        pl.semaphore_signal(
            barrier, inc=1, device_id=device(me, (y + k) % n_y), device_id_type=LOGICAL
        )

    len0, len1 = lens_ref[0], lens_ref[1]
    lane = lax.broadcasted_iota(jnp.int32, (1, 128), 1)
    id_row = jnp.full((1, 128), -1, jnp.int32)
    owner = []
    for s in range(SLOTS):
        k = s - len0
        second = jnp.where(
            k == 0, lists_ref[1, 0], jnp.where(k == 1, lists_ref[1, 1], lists_ref[1, 2])
        )
        first = lists_ref[0, min(s, 2)]
        in0 = jnp.int32(s) < len0
        in1 = k < len1
        slot_id = jnp.where(in0, first, jnp.where(in1, second, -1))
        owner.append(jnp.where(in0, 0, jnp.where(in1, 1, 2)))
        id_row = jnp.where(lane == s, slot_id, id_row)
    ids[me] = id_row

    scores = mm(q_ref[...], p_ref[...], NT)
    for g in range(n_y):
        for b in range(2):
            part_in[g, b * rows : (b + 1) * rows, :] = scores[
                b * block + g * rows : b * block + (g + 1) * rows
            ]
    for b in range(2):
        cols[0, b * block : (b + 1) * block, :] = jnp.broadcast_to(
            lg_ref[b : b + 1, :], (block, 128)
        ).T
        column = (pos_ref[b : b + 1, :] // block).astype(F32)
        cols[1, b * block : (b + 1) * block, :] = jnp.broadcast_to(column, (block, 128)).T

    pl.semaphore_wait(barrier, n_dp - 1 + n_y - 1)

    each_peer(lambda p: copy_to(ids.at[me], ids.at[me], ids_s, ids_r, device(p, y)).start())
    for k in range(1, n_y):
        g = (y + k) % n_y
        copy_to(part_in.at[g], recv_in.at[y], ri_s, ri_r, device(me, g)).start()
    wait_bytes(ids.at[pl.ds(0, n_dp - 1)], ids_r)

    id_mat = ids[...].reshape(n_dp, 128)
    number = lax.broadcasted_iota(jnp.int32, (n_dp, p_ref.shape[0]), 1)
    hots = [(id_mat[:, s : s + 1] == number).astype(F32) for s in range(SLOTS)]

    def to_messages(value, s, c):
        for h in range(2):
            wide[pl.ds(s * chunks + 2 * c + h, n_dp, stride=msg), :] = value[
                :, h * 128 : (h + 1) * 128
            ]

    def from_messages():
        for s in range(SLOTS):
            for c in range(chunks):
                listed[s * n_dp : (s + 1) * n_dp, c * 128 : (c + 1) * 128] = wide[
                    pl.ds(s * chunks + c, n_dp, stride=msg), :
                ].astype(BF16)

    step_rows = 512

    def narrow(dst):
        def step(i, carry):
            at = pl.ds(pl.multiple_of(i * step_rows, step_rows), step_rows)
            dst[at, :] = wide[at, :].astype(BF16)
            return carry

        lax.fori_loop(0, n_dp * msg // step_rows, step, 0)

    def widen(src):
        def step(i, carry):
            at = pl.ds(pl.multiple_of(i * step_rows, step_rows), step_rows)
            wide[at, :] = src[at, :].astype(F32)
            return carry

        lax.fori_loop(0, n_dp * msg // step_rows, step, 0)

    for s in range(SLOTS):
        hot = hots[s].astype(BF16)
        for c in range(chunks // 2):
            to_messages(mm(hot, p_ref[:, c * 256 : (c + 1) * 256]), s, c)
    narrow(send1)

    def at_row(ref, p):
        return ref.at[pl.ds(pl.multiple_of(p * msg, msg), msg)]

    def exchange(src, dst, ss, rs):
        far_first(
            lambda p: copy_to(at_row(src, p), at_row(dst, me), ss, rs, device(p, y)).start()
        )
        pltpu.make_async_copy(at_row(src, me), at_row(dst, me), loc).start()

    def finish(dst, rs):
        wait_bytes(dst.at[pl.ds(0, (n_dp - 1) * msg)], rs)
        wait_bytes(at_row(dst, me), loc)

    exchange(send1, recv1, e1_s, e1_r)

    for s in range(SLOTS):
        hot_t[:, s * n_dp : (s + 1) * n_dp] = hots[s].T.astype(BF16)
    recv_in[y] = part_in[y]
    wait_bytes(recv_in.at[pl.ds(0, n_y - 1)], ri_r)
    total = recv_in[0]
    for g in range(1, n_y):
        total = total + recv_in[g]
    sum_in[...] = SCALE * total

    finish(recv1, e1_r)
    widen(recv1)
    from_messages()
    scores_l = mm(q_ref[...], listed[...], NT)
    for s in range(SLOTS):
        mine = jnp.where(
            jnp.full((block, 128), owner[s]) == 1,
            scores_l[block:, s * n_dp : (s + 1) * n_dp],
            scores_l[:block, s * n_dp : (s + 1) * n_dp],
        )
        for g in range(n_y):
            part_l[g, s] = mine[g * rows : (g + 1) * rows]
    for k in range(1, n_y):
        g = (y + k) % n_y
        copy_to(part_l.at[g], recv_l.at[y], rl_s, rl_r, device(me, g)).start()
    recv_l[y] = part_l[y]

    own_cols = []
    for b in range(2):
        at = pl.ds(pl.multiple_of(b * block + y * rows, rows), rows)
        own_cols.append((cols[0, at, :][:, :1], cols[1, at, :][:, :1]))
    wait_bytes(recv_l.at[pl.ds(0, n_y - 1)], rl_r)
    slot_scores = []
    for s in range(SLOTS):
        t = recv_l[0, s]
        for g in range(1, n_y):
            t = t + recv_l[g, s]
        slot_scores.append(SCALE * t)
    logs = []
    for b in range(2):
        sc = sum_in[b * rows : (b + 1) * rows, :]
        opened = [
            jnp.where(jnp.full((rows, 128), owner[s]) == b, slot_scores[s], -jnp.inf)
            for s in range(SLOTS)
        ]
        top = jnp.max(sc, axis=1, keepdims=True)
        for o in opened:
            top = jnp.maximum(top, jnp.max(o, axis=1, keepdims=True))
        acc = jnp.sum(jnp.exp(sc - top), axis=1, keepdims=True)
        for o in opened:
            acc = acc + jnp.sum(jnp.exp(o - top), axis=1, keepdims=True)
        logs.append(top + jnp.log(acc))
    for s in range(SLOTS):
        which = jnp.full((rows, 1), owner[s])
        log_s = jnp.where(which == 1, logs[1], logs[0])
        grad_s = jnp.where(which == 1, own_cols[1][0], own_cols[0][0])
        weight = grad_s * jnp.exp(slot_scores[s] - log_s)
        weight = jnp.where(jnp.full((rows, 128), owner[s]) == 2, 0.0, weight)
        wl_all[y, s] = weight.astype(BF16)
    for k in range(1, n_y):
        g = (y + k) % n_y
        copy_to(wl_all.at[y], wl_all.at[y], al_s, al_r, device(me, g)).start()

    number_in = lax.broadcasted_iota(jnp.int32, (rows, p_ref.shape[0]), 1).astype(F32)
    ls_all[y] = jnp.zeros((8, 128), F32)
    for b in range(2):
        sc = sum_in[b * rows : (b + 1) * rows, :]
        positive = number_in == own_cols[b][1]
        loss = logs[b] - jnp.sum(jnp.where(positive, sc, 0.0), axis=1, keepdims=True)
        weight = own_cols[b][0] * (jnp.exp(sc - logs[b]) - positive.astype(F32))
        wi_all[y, b * rows : (b + 1) * rows, :] = weight.astype(BF16)
        place = lax.broadcasted_iota(jnp.int32, (rows, 128), 1) - y * rows
        diag = place == lax.broadcasted_iota(jnp.int32, (rows, 128), 0)
        ls_all[y, b : b + 1, :] = jnp.sum(jnp.where(diag, loss, 0.0), axis=0, keepdims=True)

    wait_bytes(wl_all.at[pl.ds(0, n_y - 1)], al_r)
    for s in range(SLOTS):
        w_s = jnp.concatenate([wl_all[g, s].astype(F32) for g in range(n_y)], axis=0)
        w_t = w_s.T
        for b in range(2):
            keep = jnp.where(jnp.full((block, 128), owner[s]) == b, 1.0, 0.0)
            w_full[b * block : (b + 1) * block, s * 128 : (s + 1) * 128] = (w_s * keep).astype(BF16)
            w_full_t[s * 128 : (s + 1) * 128, b * block : (b + 1) * block] = (w_t * keep).astype(BF16)
    for s in range(SLOTS):
        for c in range(chunks // 2):
            share = mm(
                w_full_t[s * 128 : (s + 1) * 128, :], q_ref[:, c * 256 : (c + 1) * 256]
            )
            to_messages(SCALE * share, s, c)
    narrow(send2)
    exchange(send2, recv2, e2_s, e2_r)

    for k in range(1, n_y):
        g = (y + k) % n_y
        copy_to(wi_all.at[y], wi_all.at[y], ai_s, ai_r, device(me, g)).start()
        copy_to(ls_all.at[y], ls_all.at[y], ls_s, ls_r, device(me, g)).start()
    wait_bytes(wi_all.at[pl.ds(0, n_y - 1)], ai_r)
    wait_bytes(ls_all.at[pl.ds(0, n_y - 1)], ls_r)
    loss_all = ls_all[0]
    for g in range(1, n_y):
        loss_all = loss_all + ls_all[g]
    loss_ref[...] = loss_all[0:2, :]
    for b in range(2):
        for g in range(n_y):
            w_in[b * block + g * rows : b * block + (g + 1) * rows, :] = wi_all[
                g, b * rows : (b + 1) * rows, :
            ]
    w_in_t = w_in[...].astype(F32).T.astype(BF16)
    for c in range(chunks // 2):
        cc = slice(c * 256, (c + 1) * 256)
        grad = mm(w_in[...], p_ref[:, cc]) + mm(w_full[...], listed[:, cc])
        gq_ref[:, cc] = (SCALE * grad).astype(BF16)
        own[:, cc] = SCALE * mm(w_in_t, q_ref[:, cc])

    finish(recv2, e2_r)
    widen(recv2)
    from_messages()
    for c in range(chunks // 2):
        cc = slice(c * 256, (c + 1) * 256)
        gp_ref[:, cc] = (own[:, cc] + mm(hot_t[...], listed[:, cc])).astype(BF16)

    wait_bytes(ids.at[pl.ds(0, n_dp - 1)], ids_s)
    wait_bytes(recv1.at[pl.ds(0, (n_dp - 1) * msg)], e1_s)
    wait_bytes(recv1.at[pl.ds(0, (n_dp - 1) * msg)], e2_s)
    wait_bytes(recv_in.at[pl.ds(0, n_y - 1)], ri_s)
    wait_bytes(recv_l.at[pl.ds(0, n_y - 1)], rl_s)
    wait_bytes(wl_all.at[pl.ds(0, n_y - 1)], al_s)
    wait_bytes(wi_all.at[pl.ds(0, n_y - 1)], ai_s)
    wait_bytes(ls_all.at[pl.ds(0, n_y - 1)], ls_s)


def per_device(z_count, queries, passages, block_lists, list_lengths, positive, loss_grad):
    n_dp, n_y = lax.axis_size("dp"), lax.axis_size("grp")
    n_blocks, shard_rows, width = passages.shape
    n_q = queries.shape[0]
    block = n_q // 2
    rows = block // n_y
    chunks = width // 128
    msg = SLOTS * chunks
    vmem = pl.BlockSpec(memory_space=pltpu.VMEM)
    smem = pl.BlockSpec(memory_space=pltpu.SMEM)
    big = (n_dp * msg, 128)
    losses, gq, gp = pl.pallas_call(
        functools.partial(kernel, z_count),
        out_shape=(
            jax.ShapeDtypeStruct((2, block), F32),
            jax.ShapeDtypeStruct((n_q, width), BF16),
            jax.ShapeDtypeStruct((n_blocks, width), BF16),
        ),
        in_specs=[vmem, vmem, smem, smem, vmem, vmem],
        out_specs=(vmem, vmem, vmem),
        scratch_shapes=[
            pltpu.VMEM((n_dp, 1, 128), jnp.int32),
            pltpu.VMEM(big, BF16),
            pltpu.VMEM(big, BF16),
            pltpu.VMEM(big, BF16),
            pltpu.VMEM(big, BF16),
            pltpu.VMEM(big, F32),
            pltpu.VMEM((SLOTS * n_dp, width), BF16),
            pltpu.VMEM((n_blocks, SLOTS * n_dp), BF16),
            pltpu.VMEM((n_y, 2 * rows, n_blocks), F32),
            pltpu.VMEM((n_y, 2 * rows, n_blocks), F32),
            pltpu.VMEM((n_y, SLOTS, rows, 128), F32),
            pltpu.VMEM((n_y, SLOTS, rows, 128), F32),
            pltpu.VMEM((2 * rows, n_blocks), F32),
            pltpu.VMEM((2, n_q, 128), F32),
            pltpu.VMEM((n_y, SLOTS, rows, 128), BF16),
            pltpu.VMEM((n_y, 2 * rows, n_blocks), BF16),
            pltpu.VMEM((n_y, 8, 128), F32),
            pltpu.VMEM((n_q, n_blocks), BF16),
            pltpu.VMEM((n_q, SLOTS * 128), BF16),
            pltpu.VMEM((SLOTS * 128, n_q), BF16),
            pltpu.VMEM((n_blocks, width), F32),
        ]
        + [pltpu.SemaphoreType.DMA] * 17,
        name="loss_and_gradients",
        compiler_params=pltpu.CompilerParams(
            collective_id=0, has_side_effects=True, vmem_limit_bytes=40 * 2**20
        ),
    )(
        queries,
        passages.reshape(n_blocks * shard_rows, width),
        block_lists,
        list_lengths,
        positive.reshape(2, block),
        loss_grad.reshape(2, block),
    )
    return losses.reshape(n_q), gq, gp.reshape(passages.shape)


def solution(mesh):
    in_specs = (P("dp", "grp"), P(None, "dp", "grp"), P("dp", None), P("dp"), P("dp"), P("dp"))
    out_specs = (P("dp"), P("dp", "grp"), P(None, "dp", "grp"))
    z_count = mesh.shape["dp"] // 8
    return jax.shard_map(
        functools.partial(per_device, z_count),
        mesh=mesh, in_specs=in_specs, out_specs=out_specs, check_vma=False,
    )
```

```python
import functools
import math

import jax
import jax.numpy as jnp
from jax import lax
from jax.experimental import pallas as pl
from jax.experimental.pallas import tpu as pltpu
from jax.sharding import PartitionSpec as P

D = 4096
SCALE = 3.0 / math.sqrt(D)
SLOTS = 4
LOGICAL = pl.DeviceIdType.LOGICAL
NN = (((1,), (0,)), ((), ()))
NT = (((1,), (1,)), ((), ()))
F32, BF16 = jnp.float32, jnp.bfloat16


def mm(a, b, dims=NN):
    return lax.dot_general(a, b, dims, preferred_element_type=F32)


def kernel(
    z_count,
    q_hbm, p_hbm, lists_hbm, lens_hbm, pos_hbm, lg_hbm,
    loss_ref, gq_ref, gp_ref,
    q_ref, p_ref, lists_ref, lens_ref, pos_ref, lg_ref,
    ids, send1, recv1, send2, recv2, wide, listed, shared, hot_t,
    part_in, recv_in, part_l, recv_l, sum_in, sum_l, cols,
    wl_all, wi_all, ls_all, w_in, w_full, w_full_t, own,
    in_s, loc, sent, ids_r, e1_r, e2_r, ri_r, rl_r, al_r, ai_r, ls_r,
):
    me = lax.axis_index("dp")
    y = lax.axis_index("grp")
    n_dp = lax.axis_size("dp")
    n_y = lax.axis_size("grp")
    plane = n_dp // z_count
    my_z, my_xc = me // plane, me % plane
    block = q_ref.shape[0] // 2
    rows = block // n_y
    chunks = q_ref.shape[1] // 128
    msg = SLOTS * chunks
    far = z_count // 2
    order = [far, far - 1, 1 - far, 0]
    for h in range(far - 2, 0, -1):
        order += [h, -h]
    opposite = [order.index(-dz) if -dz in order else order.index(dz) for dz in order]
    parts = z_count // 4
    peers = 4 * plane
    part_rows = peers * msg
    lanes = SLOTS * peers
    zs = [lax.rem(my_z + dz + z_count, z_count) for dz in order]
    base = [z * (plane * n_y) + y for z in zs]

    def copy_to(src, dst, ss, rs, dev):
        return pltpu.make_async_remote_copy(
            src_ref=src, dst_ref=dst, send_sem=ss, recv_sem=rs, device_id=dev, device_id_type=LOGICAL
        )

    def wait_bytes(ref, sem):
        pltpu.make_async_copy(ref, ref, sem).wait()

    def y_peers(body):
        for k in range(1, n_y):
            g = lax.rem(y + k, n_y)
            body(g, me * n_y + g)

    def part_peers(t, body):
        def step(k, carry):
            xc = lax.rem(my_xc + k, plane)
            for i in range(4 * t, 4 * t + 4):
                body(i * plane + xc, opposite[i] * plane + my_xc, base[i] + xc * n_y)
            return carry

        lax.fori_loop(1, plane, step, 0)
        for i in range(4 * t, 4 * t + 4):
            if order[i] != 0:
                body(i * plane + my_xc, opposite[i] * plane + my_xc, base[i] + my_xc * n_y)

    my_place = order.index(0) * plane + my_xc
    copies_in = [
        pltpu.make_async_copy(src, dst, in_s.at[k])
        for k, (src, dst) in enumerate(
            (
                (lists_hbm, lists_ref), (lens_hbm, lens_ref), (q_hbm, q_ref),
                (p_hbm, p_ref), (pos_hbm, pos_ref), (lg_hbm, lg_ref),
            )
        )
    ]
    for c in copies_in:
        c.start()

    barrier = pltpu.get_barrier_semaphore()

    def greet(dev):
        pl.semaphore_signal(barrier, inc=1, device_id=dev, device_id_type=LOGICAL)

    def greet_z(i, carry):
        z = lax.rem(my_z + i, z_count)
        for xc in range(plane):
            greet((z * plane + xc) * n_y + y)
        return carry

    lax.fori_loop(1, z_count, greet_z, 0)
    for k in range(1, plane):
        greet((my_z * plane + lax.rem(my_xc + k, plane)) * n_y + y)
    y_peers(lambda g, dev: greet(dev))

    copies_in[0].wait()
    copies_in[1].wait()
    len0, len1 = lens_ref[0], lens_ref[1]
    lane = lax.broadcasted_iota(jnp.int32, (1, 128), 1)
    id_row = jnp.full((1, 128), -1, jnp.int32)
    owner = jnp.full((1, lanes), 2, jnp.int32)
    slot_lane = lax.broadcasted_iota(jnp.int32, (1, lanes), 1) // peers
    for s in range(SLOTS):
        k = s - len0
        second = jnp.where(
            k == 0, lists_ref[1, 0], jnp.where(k == 1, lists_ref[1, 1], lists_ref[1, 2])
        )
        first = lists_ref[0, min(s, 2)]
        in0 = jnp.int32(s) < len0
        in1 = k < len1
        slot_id = jnp.where(in0, first, jnp.where(in1, second, -1))
        owner = jnp.where(slot_lane == s, jnp.where(in0, 0, jnp.where(in1, 1, 2)), owner)
        id_row = jnp.where(lane == s, slot_id, id_row)
    ids[my_place] = id_row

    for c in copies_in[2:]:
        c.wait()
    scores = mm(q_ref[...], p_ref[...], NT)
    for g in range(n_y):
        for b in range(2):
            part_in[g, b * rows : (b + 1) * rows, :] = scores[
                b * block + g * rows : b * block + (g + 1) * rows
            ]

    pl.semaphore_wait(barrier, n_dp - 1 + n_y - 1)

    for t in range(parts):
        part_peers(
            t,
            lambda i, there, dev: copy_to(
                ids.at[my_place], ids.at[there], sent.at[0], ids_r.at[t], dev
            ).start(),
        )

    def part_sizes(t):
        return peers - 1 if t == order.index(0) // 4 else peers

    def to_messages(value, t, c):
        for s in range(SLOTS):
            for h in range(2):
                wide[pl.ds(t * part_rows + s * chunks + 2 * c + h, peers, stride=msg), :] = value[
                    s * peers : (s + 1) * peers, h * 128 : (h + 1) * 128
                ]

    def narrow(dst, t):
        at = slice(t * part_rows, (t + 1) * part_rows)
        dst[at, :] = wide[at, :].astype(BF16)

    def from_messages(src, dst, t):
        at = slice(t * part_rows, (t + 1) * part_rows)
        wide[at, :] = src[at, :].astype(F32)
        for s in range(SLOTS):
            for c in range(chunks):
                dst[t * lanes + s * peers : t * lanes + (s + 1) * peers, c * 128 : (c + 1) * 128] = wide[
                    pl.ds(t * part_rows + s * chunks + c, peers, stride=msg), :
                ].astype(BF16)

    def at_row(ref, p):
        return ref.at[pl.ds(pl.multiple_of(p * msg, msg), msg)]

    def send_part(t, src, dst, ss, rs):
        part_peers(
            t,
            lambda i, there, dev: copy_to(
                at_row(src, i), at_row(dst, there), ss, rs.at[t], dev
            ).start(),
        )
        if t == order.index(0) // 4:
            pltpu.make_async_copy(at_row(src, my_place), at_row(dst, my_place), loc).start()

    def wait_part(t, dst, rs):
        wait_bytes(dst.at[pl.ds(t * part_rows, part_sizes(t) * msg)], rs.at[t])
        if t == order.index(0) // 4:
            wait_bytes(at_row(dst, my_place), loc)

    number = lax.broadcasted_iota(jnp.int32, (peers, p_ref.shape[0]), 1)
    for t in range(parts):
        wait_bytes(ids.at[pl.ds(t * peers, part_sizes(t))], ids_r.at[t])
        id_mat = ids[t * peers : (t + 1) * peers].reshape(peers, 128)
        hot = jnp.concatenate(
            [(id_mat[:, s : s + 1] == number).astype(F32) for s in range(SLOTS)], axis=0
        )
        hot_16 = hot.astype(BF16)
        for c in range(chunks // 2):
            to_messages(mm(hot_16, p_ref[:, c * 256 : (c + 1) * 256]), t, c)
        narrow(send1, t)
        send_part(t, send1, recv1, sent.at[1], e1_r)
        hot_t[:, t * lanes : (t + 1) * lanes] = hot.T.astype(BF16)

    y_peers(lambda g, dev: copy_to(part_in.at[g], recv_in.at[y], sent.at[2], ri_r, dev).start())
    for b in range(2):
        cols[0, b * block : (b + 1) * block, :] = jnp.broadcast_to(
            lg_ref[b : b + 1, :], (block, 128)
        ).T
        column = (pos_ref[b : b + 1, :] // block).astype(F32)
        cols[1, b * block : (b + 1) * block, :] = jnp.broadcast_to(column, (block, 128)).T
    recv_in[y] = part_in[y]
    wait_bytes(recv_in.at[pl.ds(0, n_y - 1)], ri_r)
    total = recv_in[0]
    for g in range(1, n_y):
        total = total + recv_in[g]
    sum_in[...] = SCALE * total

    def add_scores(t):
        wait_bytes(recv_l.at[t, pl.ds(0, n_y - 1)], rl_r.at[t])
        total = recv_l[t, 0]
        for g in range(1, n_y):
            total = total + recv_l[t, g]
        sum_l[t] = SCALE * total

    for t in range(parts):
        wait_part(t, recv1, e1_r)
        from_messages(recv1, listed, t)
        scores = mm(q_ref[...], listed[t * lanes : (t + 1) * lanes, :], NT)
        mine = jnp.where(jnp.broadcast_to(owner == 1, (block, lanes)), scores[block:], scores[:block])
        for g in range(n_y):
            part_l[t, g] = mine[g * rows : (g + 1) * rows]
        y_peers(
            lambda g, dev: copy_to(
                part_l.at[t, g], recv_l.at[t, y], sent.at[3], rl_r.at[t], dev
            ).start()
        )
        recv_l[t, y] = part_l[t, y]
        if t > 0:
            add_scores(t - 1)
    add_scores(parts - 1)

    own_cols = []
    for b in range(2):
        at = pl.ds(pl.multiple_of(b * block + y * rows, rows), rows)
        own_cols.append((cols[0, at, :][:, :1], cols[1, at, :][:, :1]))
    of_block = [jnp.broadcast_to(owner == b, (rows, lanes)) for b in range(2)]
    logs = []
    for b in range(2):
        sc = sum_in[b * rows : (b + 1) * rows, :]
        opened = [jnp.where(of_block[b], sum_l[t], -jnp.inf) for t in range(parts)]
        best = opened[0]
        for o in opened[1:]:
            best = jnp.maximum(best, o)
        top = jnp.maximum(
            jnp.max(sc, axis=1, keepdims=True), jnp.max(best, axis=1, keepdims=True)
        )
        terms = jnp.exp(opened[0] - top)
        for o in opened[1:]:
            terms = terms + jnp.exp(o - top)
        acc = jnp.sum(jnp.exp(sc - top), axis=1, keepdims=True) + jnp.sum(
            terms, axis=1, keepdims=True
        )
        logs.append(top + jnp.log(acc))
    log_l = jnp.where(of_block[1], logs[1], logs[0])
    grad_l = jnp.where(of_block[1], own_cols[1][0], own_cols[0][0])
    dead = jnp.broadcast_to(owner == 2, (rows, lanes))
    for t in range(parts):
        weight = jnp.where(dead, 0.0, grad_l * jnp.exp(sum_l[t] - log_l))
        wl_all[t, y] = weight.astype(BF16)
        y_peers(
            lambda g, dev: copy_to(
                wl_all.at[t, y], wl_all.at[t, y], sent.at[4], al_r.at[t], dev
            ).start()
        )

    number_in = lax.broadcasted_iota(jnp.int32, (rows, p_ref.shape[0]), 1).astype(F32)
    ls_all[y] = jnp.zeros((8, 128), F32)
    for b in range(2):
        sc = sum_in[b * rows : (b + 1) * rows, :]
        positive = number_in == own_cols[b][1]
        loss = logs[b] - jnp.sum(jnp.where(positive, sc, 0.0), axis=1, keepdims=True)
        weight = own_cols[b][0] * (jnp.exp(sc - logs[b]) - positive.astype(F32))
        wi_all[y, b * rows : (b + 1) * rows, :] = weight.astype(BF16)
        place = lax.broadcasted_iota(jnp.int32, (rows, 128), 1) - y * rows
        diag = place == lax.broadcasted_iota(jnp.int32, (rows, 128), 0)
        ls_all[y, b : b + 1, :] = jnp.sum(jnp.where(diag, loss, 0.0), axis=0, keepdims=True)

    for t in range(parts):
        wait_bytes(wl_all.at[t, pl.ds(0, n_y - 1)], al_r.at[t])
        w_t = jnp.concatenate([wl_all[t, g].astype(F32) for g in range(n_y)], axis=0)
        for b in range(2):
            w_b = jnp.where(jnp.broadcast_to(owner == b, (block, lanes)), w_t, 0.0)
            w_full[b * block : (b + 1) * block, t * lanes : (t + 1) * lanes] = w_b.astype(BF16)
            w_full_t[t * lanes : (t + 1) * lanes, b * block : (b + 1) * block] = w_b.T.astype(BF16)
        for c in range(chunks // 2):
            share = mm(
                w_full_t[t * lanes : (t + 1) * lanes, :], q_ref[:, c * 256 : (c + 1) * 256]
            )
            to_messages(SCALE * share, t, c)
        narrow(send2, t)
        send_part(t, send2, recv2, sent.at[5], e2_r)

    y_peers(lambda g, dev: copy_to(wi_all.at[y], wi_all.at[y], sent.at[6], ai_r, dev).start())
    y_peers(lambda g, dev: copy_to(ls_all.at[y], ls_all.at[y], sent.at[7], ls_r, dev).start())
    wait_bytes(wi_all.at[pl.ds(0, n_y - 1)], ai_r)
    wait_bytes(ls_all.at[pl.ds(0, n_y - 1)], ls_r)
    loss_all = ls_all[0]
    for g in range(1, n_y):
        loss_all = loss_all + ls_all[g]
    loss_ref[...] = loss_all[0:2, :]
    for b in range(2):
        for g in range(n_y):
            w_in[b * block + g * rows : b * block + (g + 1) * rows, :] = wi_all[
                g, b * rows : (b + 1) * rows, :
            ]
    w_in_t = w_in[...].astype(F32).T.astype(BF16)
    for c in range(chunks // 2):
        cc = slice(c * 256, (c + 1) * 256)
        grad = mm(w_in[...], p_ref[:, cc]) + mm(w_full[...], listed[:, cc])
        gq_ref[:, cc] = (SCALE * grad).astype(BF16)
        own[:, cc] = SCALE * mm(w_in_t, q_ref[:, cc])

    half = lanes * parts // 2
    for t in range(parts):
        wait_part(t, recv2, e2_r)
        from_messages(recv2, shared, t)
        if 2 * (t + 1) == parts:
            for c in range(chunks // 2):
                cc = slice(c * 256, (c + 1) * 256)
                own[:, cc] += mm(hot_t[:, :half], shared[:half, cc])
    for c in range(chunks // 2):
        cc = slice(c * 256, (c + 1) * 256)
        gp_ref[:, cc] = (own[:, cc] + mm(hot_t[:, half:], shared[half:, cc])).astype(BF16)

    wait_bytes(ids.at[pl.ds(0, n_dp - 1)], sent.at[0])
    wait_bytes(recv1.at[pl.ds(0, (n_dp - 1) * msg)], sent.at[1])
    wait_bytes(recv_in.at[pl.ds(0, n_y - 1)], sent.at[2])
    wait_bytes(recv_l.at[pl.ds(0, n_y - 1)], sent.at[3])
    wait_bytes(wl_all.at[pl.ds(0, n_y - 1)], sent.at[4])
    wait_bytes(recv2.at[pl.ds(0, (n_dp - 1) * msg)], sent.at[5])
    wait_bytes(wi_all.at[pl.ds(0, n_y - 1)], sent.at[6])
    wait_bytes(ls_all.at[pl.ds(0, n_y - 1)], sent.at[7])


def store(a, b, c, a_out, b_out, c_out, sems):
    copies = [
        pltpu.make_async_copy(src, dst, sems.at[k])
        for k, (src, dst) in enumerate(((a, a_out), (b, b_out), (c, c_out)))
    ]
    for copy in copies:
        copy.start()
    for copy in copies:
        copy.wait()


def per_device(z_count, queries, passages, block_lists, list_lengths, positive, loss_grad):
    n_dp, n_y = lax.axis_size("dp"), lax.axis_size("grp")
    n_blocks, shard_rows, width = passages.shape
    n_q = queries.shape[0]
    block = n_q // 2
    rows = block // n_y
    chunks = width // 128
    msg = SLOTS * chunks
    vmem = pl.BlockSpec(memory_space=pltpu.VMEM)
    hbm = pl.BlockSpec(memory_space=pltpu.HBM)
    parts = z_count // 4
    lanes = SLOTS * (n_dp // parts)
    big = (n_dp * msg, 128)
    losses, gq, gp = pl.pallas_call(
        functools.partial(kernel, z_count),
        out_shape=(
            pltpu.VMEM((2, block), F32),
            pltpu.VMEM((n_q, width), BF16),
            pltpu.VMEM((n_blocks, width), BF16),
        ),
        in_specs=[hbm] * 6,
        out_specs=(vmem, vmem, vmem),
        scratch_shapes=[
            pltpu.VMEM((n_q, width), BF16),
            pltpu.VMEM((n_blocks, width), BF16),
            pltpu.SMEM(block_lists.shape, jnp.int32),
            pltpu.SMEM(list_lengths.shape, jnp.int32),
            pltpu.VMEM((2, block), jnp.int32),
            pltpu.VMEM((2, block), F32),
            pltpu.VMEM((n_dp, 1, 128), jnp.int32),
            pltpu.VMEM(big, BF16),
            pltpu.VMEM(big, BF16),
            pltpu.VMEM(big, BF16),
            pltpu.VMEM(big, BF16),
            pltpu.VMEM(big, F32),
            pltpu.VMEM((SLOTS * n_dp, width), BF16),
            pltpu.VMEM((SLOTS * n_dp, width), BF16),
            pltpu.VMEM((n_blocks, SLOTS * n_dp), BF16),
            pltpu.VMEM((n_y, 2 * rows, n_blocks), F32),
            pltpu.VMEM((n_y, 2 * rows, n_blocks), F32),
            pltpu.VMEM((parts, n_y, rows, lanes), F32),
            pltpu.VMEM((parts, n_y, rows, lanes), F32),
            pltpu.VMEM((2 * rows, n_blocks), F32),
            pltpu.VMEM((parts, rows, lanes), F32),
            pltpu.VMEM((2, n_q, 128), F32),
            pltpu.VMEM((parts, n_y, rows, lanes), BF16),
            pltpu.VMEM((n_y, 2 * rows, n_blocks), BF16),
            pltpu.VMEM((n_y, 8, 128), F32),
            pltpu.VMEM((n_q, n_blocks), BF16),
            pltpu.VMEM((n_q, parts * lanes), BF16),
            pltpu.VMEM((parts * lanes, n_q), BF16),
            pltpu.VMEM((n_blocks, width), F32),
            pltpu.SemaphoreType.DMA((6,)),
            pltpu.SemaphoreType.DMA,
            pltpu.SemaphoreType.DMA((8,)),
            pltpu.SemaphoreType.DMA((parts,)),
            pltpu.SemaphoreType.DMA((parts,)),
            pltpu.SemaphoreType.DMA((parts,)),
            pltpu.SemaphoreType.DMA,
            pltpu.SemaphoreType.DMA((parts,)),
            pltpu.SemaphoreType.DMA((parts,)),
            pltpu.SemaphoreType.DMA,
            pltpu.SemaphoreType.DMA,
        ],
        name="loss_and_gradients",
        compiler_params=pltpu.CompilerParams(
            collective_id=0, has_side_effects=True, vmem_limit_bytes=40 * 2**20
        ),
    )(
        *(
            pltpu.with_memory_space_constraint(x, pltpu.HBM)
            for x in (
                queries,
                passages.reshape(n_blocks * shard_rows, width),
                block_lists,
                list_lengths,
                positive.reshape(2, block),
                loss_grad.reshape(2, block),
            )
        )
    )
    losses, gq, gp = pl.pallas_call(
        store,
        out_shape=tuple(jax.ShapeDtypeStruct(x.shape, x.dtype) for x in (losses, gq, gp)),
        in_specs=[vmem] * 3,
        out_specs=(hbm,) * 3,
        scratch_shapes=[pltpu.SemaphoreType.DMA((3,))],
        name="store",
    )(*(pltpu.with_memory_space_constraint(x, pltpu.VMEM) for x in (losses, gq, gp)))
    return losses.reshape(n_q), gq, gp.reshape(passages.shape)


def solution(mesh):
    in_specs = (P("dp", "grp"), P(None, "dp", "grp"), P("dp", None), P("dp"), P("dp"), P("dp"))
    out_specs = (P("dp"), P("dp", "grp"), P(None, "dp", "grp"))
    z_count = mesh.shape["dp"] // 8
    return jax.shard_map(
        functools.partial(per_device, z_count),
        mesh=mesh, in_specs=in_specs, out_specs=out_specs, check_vma=False,
    )
```

```python
import functools
import math

import jax
import jax.numpy as jnp
from jax import lax
from jax.experimental import pallas as pl
from jax.experimental.pallas import tpu as pltpu
from jax.sharding import PartitionSpec as P

D = 4096
SCALE = 3.0 / math.sqrt(D)
SLOTS = 4
LOGICAL = pl.DeviceIdType.LOGICAL
NN = (((1,), (0,)), ((), ()))
NT = (((1,), (1,)), ((), ()))
F32, BF16 = jnp.float32, jnp.bfloat16


def mm(a, b, dims=NN):
    return lax.dot_general(a, b, dims, preferred_element_type=F32)


def kernel(
    z_count,
    q_hbm, p_hbm, lists_hbm, lens_hbm, pos_hbm, lg_hbm,
    loss_ref, gq_ref, gp_ref,
    q_ref, p_ref, lists_ref, lens_ref, pos_ref, lg_ref,
    ids, send1, recv1, send2a, recv2a, send2b, recv2b, send2c, recv2c, wide, listed, shared, hot_t,
    part_in, recv_in, part_l, recv_l, sum_in, sum_l, cols,
    wl_all, wi_all, ls_all, w_in, w_full, w_full_t, own,
    in_s, loc, sent, ids_r, e1_r, e2_r, e2c_r, ri_r, rl_r, al_r, ai_r, ls_r,
):
    me = lax.axis_index("dp")
    y = lax.axis_index("grp")
    n_dp = lax.axis_size("dp")
    n_y = lax.axis_size("grp")
    plane = n_dp // z_count
    my_z, my_xc = me // plane, me % plane
    block = q_ref.shape[0] // 2
    rows = block // n_y
    chunks = q_ref.shape[1] // 128
    pair = 2 * chunks
    far = z_count // 2
    order = [far, far - 1, 1 - far, 0]
    for h in range(far - 2, 0, -1):
        order += [h, -h]
    opposite = [order.index(-dz) if -dz in order else order.index(dz) for dz in order]
    parts = z_count // 4
    peers = 4 * plane
    zs = [lax.rem(my_z + dz + z_count, z_count) for dz in order]
    base = [z * (plane * n_y) + y for z in zs]
    my_part = order.index(0) // 4
    my_place = order.index(0) * plane + my_xc
    first_out = [2, 0, 1, 3] if parts == 4 else list(range(parts))

    def copy_to(src, dst, ss, rs, dev):
        return pltpu.make_async_remote_copy(
            src_ref=src, dst_ref=dst, send_sem=ss, recv_sem=rs, device_id=dev, device_id_type=LOGICAL
        )

    def wait_bytes(ref, sem):
        pltpu.make_async_copy(ref, ref, sem).wait()

    def y_peers(body):
        for k in range(1, n_y):
            g = lax.rem(y + k, n_y)
            body(g, me * n_y + g)

    def part_peers(t, body):
        def step(k, carry):
            xc = lax.rem(my_xc + k, plane)
            for i in range(4 * t, 4 * t + 4):
                body(i * plane + xc, opposite[i] * plane + my_xc, base[i] + xc * n_y)
            return carry

        lax.fori_loop(1, plane, step, 0)
        for i in range(4 * t, 4 * t + 4):
            if order[i] != 0:
                body(i * plane + my_xc, opposite[i] * plane + my_xc, base[i] + my_xc * n_y)

    def part_sizes(t):
        return peers - 1 if t == my_part else peers

    barrier = pltpu.get_barrier_semaphore()

    def greet(dev):
        pl.semaphore_signal(barrier, inc=1, device_id=dev, device_id_type=LOGICAL)

    for i, dz in enumerate(order):
        if dz != 0:
            for xc in range(plane):
                greet(base[i] + xc * n_y)
    for k in range(1, plane):
        greet(base[order.index(0)] + lax.rem(my_xc + k, plane) * n_y)
    y_peers(lambda g, dev: greet(dev))

    copies_in = [
        pltpu.make_async_copy(src, dst, in_s.at[k])
        for k, (src, dst) in enumerate(
            (
                (lists_hbm, lists_ref), (lens_hbm, lens_ref), (q_hbm, q_ref),
                (p_hbm, p_ref), (pos_hbm, pos_ref), (lg_hbm, lg_ref),
            )
        )
    ]
    for c in copies_in:
        c.start()

    copies_in[0].wait()
    copies_in[1].wait()
    len0, len1 = lens_ref[0], lens_ref[1]
    swap = len1 < len0
    early = jnp.where(swap, 1, 0)
    len_a, len_b = jnp.where(swap, len1, len0), jnp.where(swap, len0, len1)
    list_a = [jnp.where(swap, lists_ref[1, k], lists_ref[0, k]) for k in range(3)]
    list_b = [jnp.where(swap, lists_ref[0, k], lists_ref[1, k]) for k in range(3)]
    lane = lax.broadcasted_iota(jnp.int32, (1, 128), 1)
    id_row = jnp.full((1, 128), -1, jnp.int32)
    rank = []
    for s in range(SLOTS):
        k = s - len_a
        id_b = jnp.where(k == 0, list_b[0], jnp.where(k == 1, list_b[1], list_b[2]))
        in_a = jnp.int32(s) < len_a
        in_b = k < len_b
        slot_id = jnp.where(in_a, list_a[min(s, 2)], jnp.where(in_b, id_b, -1))
        rank.append(jnp.where(in_a, 0, jnp.where(in_b, 1, 2)))
        id_row = jnp.where(lane == s, slot_id, id_row)
    owner = [jnp.where(r == 0, early, jnp.where(r == 1, 1 - early, 2)) for r in rank]
    ids[my_place] = id_row

    for c in copies_in[2:]:
        c.wait()
    scores = mm(q_ref[...], p_ref[...], NT)
    for g in range(n_y):
        for b in range(2):
            part_in[g, b * rows : (b + 1) * rows, :] = scores[
                b * block + g * rows : b * block + (g + 1) * rows
            ]

    pl.semaphore_wait(barrier, n_dp - 1 + n_y - 1)

    for t in first_out:
        part_peers(
            t,
            lambda i, there, dev: copy_to(
                ids.at[my_place], ids.at[there], sent.at[0], ids_r.at[t], dev
            ).start(),
        )

    def to_messages(value, first, n, size, c):
        for h in range(2):
            wide[pl.ds(first + 2 * c + h, n, stride=size), :] = value[:, h * 128 : (h + 1) * 128]

    def from_messages(dst, first, n, size, row):
        for c in range(chunks):
            dst[row : row + n, c * 128 : (c + 1) * 128] = wide[
                pl.ds(first + c, n, stride=size), :
            ].astype(BF16)

    def at_row(ref, p):
        return ref.at[pl.ds(pl.multiple_of(p * pair, pair), pair)]

    def slab(ref, h):
        return ref.at[pl.ds(h * n_dp * pair, n_dp * pair)]

    number = lax.broadcasted_iota(jnp.int32, (peers, p_ref.shape[0]), 1)
    for h in range(2):
        src, dst = slab(send1, h), slab(recv1, h)
        for t in first_out:
            if h == 0:
                wait_bytes(ids.at[pl.ds(t * peers, part_sizes(t))], ids_r.at[t])
            id_mat = ids[t * peers : (t + 1) * peers].reshape(peers, 128)
            hot = jnp.concatenate(
                [(id_mat[:, s : s + 1] == number).astype(F32) for s in (2 * h, 2 * h + 1)], axis=0
            ).astype(BF16)
            first = (h * n_dp + t * peers) * pair
            for c in range(chunks // 2):
                value = mm(hot, p_ref[:, c * 256 : (c + 1) * 256])
                for k in range(2):
                    to_messages(value[k * peers : (k + 1) * peers], first + k * chunks, peers, pair, c)
            at = slice(first, first + peers * pair)
            send1[at, :] = wide[at, :].astype(BF16)
            part_peers(
                t,
                lambda i, there, dev: copy_to(
                    at_row(src, i), at_row(dst, there), sent.at[1 + h], e1_r.at[h], dev
                ).start(),
            )
        pltpu.make_async_copy(at_row(src, my_place), at_row(dst, my_place), loc.at[h]).start()

    y_peers(lambda g, dev: copy_to(part_in.at[g], recv_in.at[y], sent.at[3], ri_r, dev).start())
    for b in range(2):
        cols[0, b * block : (b + 1) * block, :] = jnp.broadcast_to(
            lg_ref[b : b + 1, :], (block, 128)
        ).T
        column = (pos_ref[b : b + 1, :] // block).astype(F32)
        cols[1, b * block : (b + 1) * block, :] = jnp.broadcast_to(column, (block, 128)).T
    id_mat = ids[...].reshape(n_dp, 128)
    number = lax.broadcasted_iota(jnp.int32, (n_dp, p_ref.shape[0]), 1)
    for s in range(SLOTS):
        hot_t[:, s * n_dp : (s + 1) * n_dp] = (id_mat[:, s : s + 1] == number).astype(F32).T.astype(BF16)
    recv_in[y] = part_in[y]
    wait_bytes(recv_in.at[pl.ds(0, n_y - 1)], ri_r)
    total = recv_in[0]
    for g in range(1, n_y):
        total = total + recv_in[g]
    sum_in[...] = SCALE * total
    own_cols = []
    for b in range(2):
        at = pl.ds(pl.multiple_of(b * block + y * rows, rows), rows)
        own_cols.append((cols[0, at, :][:, :1], cols[1, at, :][:, :1]))

    def listed_scores(h):
        got = slab(recv1, h)
        wait_bytes(got.at[pl.ds(0, (n_dp - 1) * pair)], e1_r.at[h])
        wait_bytes(at_row(got, my_place), loc.at[h])
        at = slice(h * n_dp * pair, (h + 1) * n_dp * pair)
        wide[at, :] = recv1[at, :].astype(F32)
        for k in range(2):
            from_messages(listed, h * n_dp * pair + k * chunks, n_dp, pair, (2 * h + k) * n_dp)
        scores = mm(q_ref[...], listed[2 * h * n_dp : 2 * (h + 1) * n_dp, :], NT)
        for k in range(2):
            of_1 = jnp.full((block, n_dp), owner[2 * h + k]) == 1
            cc = slice(k * n_dp, (k + 1) * n_dp)
            mine = jnp.where(of_1, scores[block:, cc], scores[:block, cc])
            for g in range(n_y):
                part_l[h, g, k] = mine[g * rows : (g + 1) * rows]
        y_peers(
            lambda g, dev: copy_to(
                part_l.at[h, g], recv_l.at[h, y], sent.at[4], rl_r.at[h], dev
            ).start()
        )
        recv_l[h, y] = part_l[h, y]
        wait_bytes(recv_l.at[h, pl.ds(0, n_y - 1)], rl_r.at[h])
        for k in range(2):
            total = recv_l[h, 0, k]
            for g in range(1, n_y):
                total = total + recv_l[h, g, k]
            sum_l[2 * h + k] = SCALE * total

    def pick(which, a, b):
        return jnp.where(jnp.full(a.shape, which) == 1, b, a)

    def log_total(r, slots):
        blk = early if r == 0 else 1 - early
        sc = pick(blk, sum_in[:rows, :], sum_in[rows:, :])
        opened = [
            jnp.where(jnp.full((rows, n_dp), rank[s]) == r, sum_l[s], -jnp.inf) for s in slots
        ]
        best = opened[0]
        for o in opened[1:]:
            best = jnp.maximum(best, o)
        top = jnp.maximum(
            jnp.max(sc, axis=1, keepdims=True), jnp.max(best, axis=1, keepdims=True)
        )
        terms = jnp.exp(opened[0] - top)
        for o in opened[1:]:
            terms = terms + jnp.exp(o - top)
        acc = jnp.sum(jnp.exp(sc - top), axis=1, keepdims=True) + jnp.sum(
            terms, axis=1, keepdims=True
        )
        return top + jnp.log(acc)

    grads = [
        pick(early, own_cols[0][0], own_cols[1][0]),
        pick(1 - early, own_cols[0][0], own_cols[1][0]),
    ]

    def listed_weights(s, logs):
        log_s = pick(rank[s], logs[0], logs[-1])
        grad_s = pick(rank[s], grads[0], grads[1])
        weight = grad_s * jnp.exp(sum_l[s] - log_s)
        weight = jnp.where(jnp.full((rows, n_dp), rank[s]) == 2, 0.0, weight)
        wl_all[s, y] = weight.astype(BF16)
        y_peers(
            lambda g, dev: copy_to(
                wl_all.at[s, y], wl_all.at[s, y], sent.at[5], al_r.at[s], dev
            ).start()
        )

    def shares(s, first, size):
        wait_bytes(wl_all.at[s, pl.ds(0, n_y - 1)], al_r.at[s])
        w_s = jnp.concatenate([wl_all[s, g].astype(F32) for g in range(n_y)], axis=0)
        for b in range(2):
            w_b = jnp.where(jnp.full((block, n_dp), owner[s]) == b, w_s, 0.0)
            w_full[b * block : (b + 1) * block, s * n_dp : (s + 1) * n_dp] = w_b.astype(BF16)
            w_full_t[s * n_dp : (s + 1) * n_dp, b * block : (b + 1) * block] = w_b.T.astype(BF16)
        for c in range(chunks // 2):
            share = mm(
                w_full_t[s * n_dp : (s + 1) * n_dp, :], q_ref[:, c * 256 : (c + 1) * 256]
            )
            to_messages(SCALE * share, first, n_dp, size, c)

    def send_slot(src, dst, ss, rs, own_sem):
        src[...] = wide[: n_dp * chunks, :].reshape(n_dp, chunks, 128).astype(BF16)
        for t in range(parts):
            part_peers(
                t,
                lambda i, there, dev: copy_to(src.at[i], dst.at[there], ss, rs, dev).start(),
            )
        pltpu.make_async_copy(src.at[my_place], dst.at[my_place], own_sem).start()

    listed_scores(0)
    log_a = log_total(0, (0, 1))
    listed_weights(0, (log_a,))
    shares(0, 0, chunks)
    wait_bytes(slab(recv1, 0).at[pl.ds(0, (n_dp - 1) * pair)], sent.at[1])
    wait_bytes(slab(recv1, 1).at[pl.ds(0, (n_dp - 1) * pair)], sent.at[2])
    send_slot(send2a, recv2a, sent.at[6], e2_r.at[0], loc.at[2])

    listed_scores(1)
    log_b = log_total(1, (1, 2, 3))
    for s in range(1, SLOTS):
        listed_weights(s, (log_a, log_b))
    shares(1, 0, chunks)
    send_slot(send2b, recv2b, sent.at[7], e2_r.at[1], loc.at[3])
    shares(2, 0, pair)
    shares(3, chunks, pair)
    send2c[...] = wide[: n_dp * pair, :].astype(BF16)
    for t in range(parts):
        part_peers(
            t,
            lambda i, there, dev: copy_to(
                at_row(send2c, i), at_row(recv2c, there), sent.at[8], e2c_r.at[t], dev
            ).start(),
        )
    pltpu.make_async_copy(at_row(send2c, my_place), at_row(recv2c, my_place), loc.at[4]).start()

    number_in = lax.broadcasted_iota(jnp.int32, (rows, p_ref.shape[0]), 1).astype(F32)
    ls_all[y] = jnp.zeros((8, 128), F32)
    for b in range(2):
        log_q = pick(early, log_a, log_b) if b == 0 else pick(early, log_b, log_a)
        sc = sum_in[b * rows : (b + 1) * rows, :]
        positive = number_in == own_cols[b][1]
        loss = log_q - jnp.sum(jnp.where(positive, sc, 0.0), axis=1, keepdims=True)
        weight = own_cols[b][0] * (jnp.exp(sc - log_q) - positive.astype(F32))
        wi_all[y, b * rows : (b + 1) * rows, :] = weight.astype(BF16)
        place = lax.broadcasted_iota(jnp.int32, (rows, 128), 1) - y * rows
        diag = place == lax.broadcasted_iota(jnp.int32, (rows, 128), 0)
        ls_all[y, b : b + 1, :] = jnp.sum(jnp.where(diag, loss, 0.0), axis=0, keepdims=True)
    y_peers(lambda g, dev: copy_to(wi_all.at[y], wi_all.at[y], sent.at[9], ai_r, dev).start())
    y_peers(lambda g, dev: copy_to(ls_all.at[y], ls_all.at[y], sent.at[10], ls_r, dev).start())
    wait_bytes(wi_all.at[pl.ds(0, n_y - 1)], ai_r)
    wait_bytes(ls_all.at[pl.ds(0, n_y - 1)], ls_r)
    loss_all = ls_all[0]
    for g in range(1, n_y):
        loss_all = loss_all + ls_all[g]
    loss_ref[...] = loss_all[0:2, :]
    for b in range(2):
        for g in range(n_y):
            w_in[b * block + g * rows : b * block + (g + 1) * rows, :] = wi_all[
                g, b * rows : (b + 1) * rows, :
            ]
    w_in_t = w_in[...].astype(F32).T.astype(BF16)
    for c in range(chunks // 2):
        cc = slice(c * 256, (c + 1) * 256)
        grad = mm(w_in[...], p_ref[:, cc]) + mm(w_full[...], listed[:, cc])
        gq_ref[:, cc] = (SCALE * grad).astype(BF16)
        own[:, cc] = SCALE * mm(w_in_t, q_ref[:, cc])

    for s, (src, own_sem) in enumerate(((recv2a, loc.at[2]), (recv2b, loc.at[3]))):
        wait_bytes(src.at[pl.ds(0, n_dp - 1)], e2_r.at[s])
        wait_bytes(src.at[my_place], own_sem)
        wide[: n_dp * chunks, :] = src[...].astype(F32).reshape(n_dp * chunks, 128)
        from_messages(shared, 0, n_dp, chunks, s * n_dp)
        for c in range(chunks // 2):
            cc = slice(c * 256, (c + 1) * 256)
            own[:, cc] += mm(
                hot_t[:, s * n_dp : (s + 1) * n_dp], shared[s * n_dp : (s + 1) * n_dp, cc]
            )
    for t in range(parts):
        wait_bytes(recv2c.at[pl.ds(t * peers * pair, part_sizes(t) * pair)], e2c_r.at[t])
        if t == my_part:
            wait_bytes(at_row(recv2c, my_place), loc.at[4])
        at = slice(t * peers * pair, (t + 1) * peers * pair)
        wide[at, :] = recv2c[at, :].astype(F32)
        for k in range(2):
            from_messages(
                shared, t * peers * pair + k * chunks, peers, pair, (2 + k) * n_dp + t * peers
            )
    for c in range(chunks // 2):
        cc = slice(c * 256, (c + 1) * 256)
        total = own[:, cc] + mm(hot_t[:, 2 * n_dp :], shared[2 * n_dp :, cc])
        gp_ref[:, cc] = total.astype(BF16)

    wait_bytes(ids.at[pl.ds(0, n_dp - 1)], sent.at[0])
    wait_bytes(recv_in.at[pl.ds(0, n_y - 1)], sent.at[3])
    wait_bytes(recv_l.at[:, pl.ds(0, n_y - 1)], sent.at[4])
    wait_bytes(wl_all.at[:, pl.ds(0, n_y - 1)], sent.at[5])
    wait_bytes(recv2a.at[pl.ds(0, n_dp - 1)], sent.at[6])
    wait_bytes(recv2b.at[pl.ds(0, n_dp - 1)], sent.at[7])
    wait_bytes(recv2c.at[pl.ds(0, (n_dp - 1) * pair)], sent.at[8])
    wait_bytes(wi_all.at[pl.ds(0, n_y - 1)], sent.at[9])
    wait_bytes(ls_all.at[pl.ds(0, n_y - 1)], sent.at[10])


def store(a, b, c, a_out, b_out, c_out, sems):
    copies = [
        pltpu.make_async_copy(src, dst, sems.at[k])
        for k, (src, dst) in enumerate(((a, a_out), (b, b_out), (c, c_out)))
    ]
    for copy in copies:
        copy.start()
    for copy in copies:
        copy.wait()


def per_device(z_count, queries, passages, block_lists, list_lengths, positive, loss_grad):
    n_dp, n_y = lax.axis_size("dp"), lax.axis_size("grp")
    n_blocks, shard_rows, width = passages.shape
    n_q = queries.shape[0]
    block = n_q // 2
    rows = block // n_y
    chunks = width // 128
    msg = SLOTS * chunks
    vmem = pl.BlockSpec(memory_space=pltpu.VMEM)
    hbm = pl.BlockSpec(memory_space=pltpu.HBM)
    parts = z_count // 4
    big = (n_dp * msg, 128)
    losses, gq, gp = pl.pallas_call(
        functools.partial(kernel, z_count),
        out_shape=(
            pltpu.VMEM((2, block), F32),
            pltpu.VMEM((n_q, width), BF16),
            pltpu.VMEM((n_blocks, width), BF16),
        ),
        in_specs=[hbm] * 6,
        out_specs=(vmem, vmem, vmem),
        scratch_shapes=[
            pltpu.VMEM((n_q, width), BF16),
            pltpu.VMEM((n_blocks, width), BF16),
            pltpu.SMEM(block_lists.shape, jnp.int32),
            pltpu.SMEM(list_lengths.shape, jnp.int32),
            pltpu.VMEM((2, block), jnp.int32),
            pltpu.VMEM((2, block), F32),
            pltpu.VMEM((n_dp, 1, 128), jnp.int32),
            pltpu.VMEM(big, BF16),
            pltpu.VMEM(big, BF16),
            pltpu.VMEM((n_dp, chunks, 128), BF16),
            pltpu.VMEM((n_dp, chunks, 128), BF16),
            pltpu.VMEM((n_dp, chunks, 128), BF16),
            pltpu.VMEM((n_dp, chunks, 128), BF16),
            pltpu.VMEM((n_dp * 2 * chunks, 128), BF16),
            pltpu.VMEM((n_dp * 2 * chunks, 128), BF16),
            pltpu.VMEM(big, F32),
            pltpu.VMEM((SLOTS * n_dp, width), BF16),
            pltpu.VMEM((SLOTS * n_dp, width), BF16),
            pltpu.VMEM((n_blocks, SLOTS * n_dp), BF16),
            pltpu.VMEM((n_y, 2 * rows, n_blocks), F32),
            pltpu.VMEM((n_y, 2 * rows, n_blocks), F32),
            pltpu.VMEM((2, n_y, 2, rows, n_dp), F32),
            pltpu.VMEM((2, n_y, 2, rows, n_dp), F32),
            pltpu.VMEM((2 * rows, n_blocks), F32),
            pltpu.VMEM((SLOTS, rows, n_dp), F32),
            pltpu.VMEM((2, n_q, 128), F32),
            pltpu.VMEM((SLOTS, n_y, rows, n_dp), BF16),
            pltpu.VMEM((n_y, 2 * rows, n_blocks), BF16),
            pltpu.VMEM((n_y, 8, 128), F32),
            pltpu.VMEM((n_q, n_blocks), BF16),
            pltpu.VMEM((n_q, SLOTS * n_dp), BF16),
            pltpu.VMEM((SLOTS * n_dp, n_q), BF16),
            pltpu.VMEM((n_blocks, width), F32),
            pltpu.SemaphoreType.DMA((6,)),
            pltpu.SemaphoreType.DMA((5,)),
            pltpu.SemaphoreType.DMA((11,)),
            pltpu.SemaphoreType.DMA((parts,)),
            pltpu.SemaphoreType.DMA((2,)),
            pltpu.SemaphoreType.DMA((2,)),
            pltpu.SemaphoreType.DMA((parts,)),
            pltpu.SemaphoreType.DMA,
            pltpu.SemaphoreType.DMA((2,)),
            pltpu.SemaphoreType.DMA((SLOTS,)),
            pltpu.SemaphoreType.DMA,
            pltpu.SemaphoreType.DMA,
        ],
        name="loss_and_gradients",
        compiler_params=pltpu.CompilerParams(
            collective_id=0, has_side_effects=True, vmem_limit_bytes=40 * 2**20
        ),
    )(
        *(
            pltpu.with_memory_space_constraint(x, pltpu.HBM)
            for x in (
                queries,
                passages.reshape(n_blocks * shard_rows, width),
                block_lists,
                list_lengths,
                positive.reshape(2, block),
                loss_grad.reshape(2, block),
            )
        )
    )
    losses, gq, gp = pl.pallas_call(
        store,
        out_shape=tuple(jax.ShapeDtypeStruct(x.shape, x.dtype) for x in (losses, gq, gp)),
        in_specs=[vmem] * 3,
        out_specs=(hbm,) * 3,
        scratch_shapes=[pltpu.SemaphoreType.DMA((3,))],
        name="store",
    )(*(pltpu.with_memory_space_constraint(x, pltpu.VMEM) for x in (losses, gq, gp)))
    return losses.reshape(n_q), gq, gp.reshape(passages.shape)


def solution(mesh):
    in_specs = (P("dp", "grp"), P(None, "dp", "grp"), P("dp", None), P("dp"), P("dp"), P("dp"))
    out_specs = (P("dp"), P("dp", "grp"), P(None, "dp", "grp"))
    z_count = mesh.shape["dp"] // 8
    return jax.shard_map(
        functools.partial(per_device, z_count),
        mesh=mesh, in_specs=in_specs, out_specs=out_specs, check_vma=False,
    )
```

```python
import functools
import math

import jax
import jax.numpy as jnp
from jax import lax
from jax.experimental import pallas as pl
from jax.experimental.pallas import tpu as pltpu
from jax.sharding import PartitionSpec as P

D = 4096
SCALE = 3.0 / math.sqrt(D)
SLOTS = 4
LOGICAL = pl.DeviceIdType.LOGICAL
NN = (((1,), (0,)), ((), ()))
NT = (((1,), (1,)), ((), ()))
F32, BF16 = jnp.float32, jnp.bfloat16


def mm(a, b, dims=NN):
    return lax.dot_general(a, b, dims, preferred_element_type=F32)


def kernel(
    z_count,
    q_hbm, p_hbm, lists_hbm, lens_hbm, pos_hbm, lg_hbm,
    loss_ref, gq_ref, gp_ref,
    q_ref, p_ref, lists_ref, lens_ref, pos_ref, lg_ref,
    ids, send1, recv1, send2a, recv2a, send2b, recv2b, send2c, recv2c, wide, listed, shared, hot_t,
    part_in, recv_in, part_l, recv_l, sum_in, sum_l, cols,
    wl_all, wi_all, ls_all, w_in, w_full, w_full_t, own,
    in_s, loc, sent, ids_r, e1_r, e2_r, e2c_r, ri_r, rl_r, al_r, ai_r, ls_r,
):
    me = lax.axis_index("dp")
    y = lax.axis_index("grp")
    n_dp = lax.axis_size("dp")
    n_y = lax.axis_size("grp")
    plane = n_dp // z_count
    my_z, my_xc = me // plane, me % plane
    block = q_ref.shape[0] // 2
    rows = block // n_y
    chunks = q_ref.shape[1] // 128
    pair = 2 * chunks
    far = z_count // 2
    order = [far, far - 1, 1 - far, 0]
    for h in range(far - 2, 0, -1):
        order += [h, -h]
    opposite = [order.index(-dz) if -dz in order else order.index(dz) for dz in order]
    parts = z_count // 4
    peers = 4 * plane
    zs = [lax.rem(my_z + dz + z_count, z_count) for dz in order]
    base = [z * (plane * n_y) + y for z in zs]
    my_part = order.index(0) // 4
    my_place = order.index(0) * plane + my_xc
    first_out = [2, 0, 1, 3] if parts == 4 else list(range(parts))

    def copy_to(src, dst, ss, rs, dev):
        return pltpu.make_async_remote_copy(
            src_ref=src, dst_ref=dst, send_sem=ss, recv_sem=rs, device_id=dev, device_id_type=LOGICAL
        )

    def wait_bytes(ref, sem):
        pltpu.make_async_copy(ref, ref, sem).wait()

    def y_peers(body):
        for k in range(1, n_y):
            g = lax.rem(y + k, n_y)
            body(g, me * n_y + g)

    def part_peers(t, body):
        def step(k, carry):
            xc = lax.rem(my_xc + k, plane)
            for i in range(4 * t, 4 * t + 4):
                body(i * plane + xc, opposite[i] * plane + my_xc, base[i] + xc * n_y)
            return carry

        lax.fori_loop(1, plane, step, 0)
        for i in range(4 * t, 4 * t + 4):
            if order[i] != 0:
                body(i * plane + my_xc, opposite[i] * plane + my_xc, base[i] + my_xc * n_y)

    def part_sizes(t):
        return peers - 1 if t == my_part else peers

    copies_in = [
        pltpu.make_async_copy(src, dst, in_s.at[k])
        for k, (src, dst) in enumerate(
            (
                (lists_hbm, lists_ref), (lens_hbm, lens_ref), (q_hbm, q_ref),
                (p_hbm, p_ref), (pos_hbm, pos_ref), (lg_hbm, lg_ref),
            )
        )
    ]
    for c in copies_in[:2]:
        c.start()

    barrier = pltpu.get_barrier_semaphore()

    def greet(dev):
        pl.semaphore_signal(barrier, inc=1, device_id=dev, device_id_type=LOGICAL)

    for i, dz in enumerate(order):
        if dz != 0:
            for xc in range(plane):
                greet(base[i] + xc * n_y)
    for k in range(1, plane):
        greet(base[order.index(0)] + lax.rem(my_xc + k, plane) * n_y)
    y_peers(lambda g, dev: greet(dev))
    for c in copies_in[2:]:
        c.start()


    copies_in[0].wait()
    copies_in[1].wait()
    len0, len1 = lens_ref[0], lens_ref[1]
    swap = len1 < len0
    early = jnp.where(swap, 1, 0)
    len_a, len_b = jnp.where(swap, len1, len0), jnp.where(swap, len0, len1)
    list_a = [jnp.where(swap, lists_ref[1, k], lists_ref[0, k]) for k in range(3)]
    list_b = [jnp.where(swap, lists_ref[0, k], lists_ref[1, k]) for k in range(3)]
    lane = lax.broadcasted_iota(jnp.int32, (1, 128), 1)
    id_row = jnp.full((1, 128), -1, jnp.int32)
    rank = []
    for s in range(SLOTS):
        k = s - len_a
        id_b = jnp.where(k == 0, list_b[0], jnp.where(k == 1, list_b[1], list_b[2]))
        in_a = jnp.int32(s) < len_a
        in_b = k < len_b
        slot_id = jnp.where(in_a, list_a[min(s, 2)], jnp.where(in_b, id_b, -1))
        rank.append(jnp.where(in_a, 0, jnp.where(in_b, 1, 2)))
        id_row = jnp.where(lane == s, slot_id, id_row)
    owner = [jnp.where(r == 0, early, jnp.where(r == 1, 1 - early, 2)) for r in rank]
    ids[my_place] = id_row

    pl.semaphore_wait(barrier, n_dp - 1 + n_y - 1)

    for t in first_out:
        part_peers(
            t,
            lambda i, there, dev: copy_to(
                ids.at[my_place], ids.at[there], sent.at[0], ids_r.at[t], dev
            ).start(),
        )

    def to_messages(value, first, n, size, c):
        for h in range(2):
            wide[pl.ds(first + 2 * c + h, n, stride=size), :] = value[:, h * 128 : (h + 1) * 128]

    def from_messages(dst, first, n, size, row):
        for c in range(chunks):
            dst[row : row + n, c * 128 : (c + 1) * 128] = wide[
                pl.ds(first + c, n, stride=size), :
            ].astype(BF16)

    def at_row(ref, p):
        return ref.at[pl.ds(pl.multiple_of(p * pair, pair), pair)]

    def slab(ref, h):
        return ref.at[pl.ds(h * n_dp * pair, n_dp * pair)]

    copies_in[3].wait()
    number = lax.broadcasted_iota(jnp.int32, (peers, p_ref.shape[0]), 1)
    for h in range(2):
        src, dst = slab(send1, h), slab(recv1, h)
        for t in first_out:
            if h == 0:
                wait_bytes(ids.at[pl.ds(t * peers, part_sizes(t))], ids_r.at[t])
            id_mat = ids[t * peers : (t + 1) * peers].reshape(peers, 128)
            hot = jnp.concatenate(
                [(id_mat[:, s : s + 1] == number).astype(F32) for s in (2 * h, 2 * h + 1)], axis=0
            ).astype(BF16)
            first = (h * n_dp + t * peers) * pair
            for c in range(chunks // 2):
                value = mm(hot, p_ref[:, c * 256 : (c + 1) * 256])
                for k in range(2):
                    to_messages(value[k * peers : (k + 1) * peers], first + k * chunks, peers, pair, c)
            at = slice(first, first + peers * pair)
            send1[at, :] = wide[at, :].astype(BF16)
            part_peers(
                t,
                lambda i, there, dev: copy_to(
                    at_row(src, i), at_row(dst, there), sent.at[1 + h], e1_r.at[h], dev
                ).start(),
            )
        pltpu.make_async_copy(at_row(src, my_place), at_row(dst, my_place), loc.at[h]).start()

    copies_in[2].wait()
    for c in copies_in[4:]:
        c.wait()
    scores = mm(q_ref[...], p_ref[...], NT)
    for g in range(n_y):
        for b in range(2):
            part_in[g, b * rows : (b + 1) * rows, :] = scores[
                b * block + g * rows : b * block + (g + 1) * rows
            ]
    y_peers(lambda g, dev: copy_to(part_in.at[g], recv_in.at[y], sent.at[3], ri_r, dev).start())
    for b in range(2):
        cols[0, b * block : (b + 1) * block, :] = jnp.broadcast_to(
            lg_ref[b : b + 1, :], (block, 128)
        ).T
        column = (pos_ref[b : b + 1, :] // block).astype(F32)
        cols[1, b * block : (b + 1) * block, :] = jnp.broadcast_to(column, (block, 128)).T
    id_mat = ids[...].reshape(n_dp, 128)
    number = lax.broadcasted_iota(jnp.int32, (n_dp, p_ref.shape[0]), 1)
    for s in range(SLOTS):
        hot_t[:, s * n_dp : (s + 1) * n_dp] = (id_mat[:, s : s + 1] == number).astype(F32).T.astype(BF16)
    recv_in[y] = part_in[y]
    wait_bytes(recv_in.at[pl.ds(0, n_y - 1)], ri_r)
    total = recv_in[0]
    for g in range(1, n_y):
        total = total + recv_in[g]
    sum_in[...] = SCALE * total
    own_cols = []
    for b in range(2):
        at = pl.ds(pl.multiple_of(b * block + y * rows, rows), rows)
        own_cols.append((cols[0, at, :][:, :1], cols[1, at, :][:, :1]))

    def listed_scores(h):
        got = slab(recv1, h)
        wait_bytes(got.at[pl.ds(0, (n_dp - 1) * pair)], e1_r.at[h])
        wait_bytes(at_row(got, my_place), loc.at[h])
        at = slice(h * n_dp * pair, (h + 1) * n_dp * pair)
        wide[at, :] = recv1[at, :].astype(F32)
        for k in range(2):
            from_messages(listed, h * n_dp * pair + k * chunks, n_dp, pair, (2 * h + k) * n_dp)
        scores = mm(q_ref[...], listed[2 * h * n_dp : 2 * (h + 1) * n_dp, :], NT)
        for k in range(2):
            of_1 = jnp.full((block, n_dp), owner[2 * h + k]) == 1
            cc = slice(k * n_dp, (k + 1) * n_dp)
            mine = jnp.where(of_1, scores[block:, cc], scores[:block, cc])
            for g in range(n_y):
                part_l[h, g, k] = mine[g * rows : (g + 1) * rows]
        y_peers(
            lambda g, dev: copy_to(
                part_l.at[h, g], recv_l.at[h, y], sent.at[4], rl_r.at[h], dev
            ).start()
        )
        recv_l[h, y] = part_l[h, y]
        wait_bytes(recv_l.at[h, pl.ds(0, n_y - 1)], rl_r.at[h])
        for k in range(2):
            total = recv_l[h, 0, k]
            for g in range(1, n_y):
                total = total + recv_l[h, g, k]
            sum_l[2 * h + k] = SCALE * total

    def pick(which, a, b):
        return jnp.where(jnp.full(a.shape, which) == 1, b, a)

    def log_total(r, slots):
        blk = early if r == 0 else 1 - early
        sc = pick(blk, sum_in[:rows, :], sum_in[rows:, :])
        opened = [
            jnp.where(jnp.full((rows, n_dp), rank[s]) == r, sum_l[s], -jnp.inf) for s in slots
        ]
        best = opened[0]
        for o in opened[1:]:
            best = jnp.maximum(best, o)
        top = jnp.maximum(
            jnp.max(sc, axis=1, keepdims=True), jnp.max(best, axis=1, keepdims=True)
        )
        terms = jnp.exp(opened[0] - top)
        for o in opened[1:]:
            terms = terms + jnp.exp(o - top)
        acc = jnp.sum(jnp.exp(sc - top), axis=1, keepdims=True) + jnp.sum(
            terms, axis=1, keepdims=True
        )
        return top + jnp.log(acc)

    grads = [
        pick(early, own_cols[0][0], own_cols[1][0]),
        pick(1 - early, own_cols[0][0], own_cols[1][0]),
    ]

    def listed_weights(s, logs):
        log_s = pick(rank[s], logs[0], logs[-1])
        grad_s = pick(rank[s], grads[0], grads[1])
        weight = grad_s * jnp.exp(sum_l[s] - log_s)
        weight = jnp.where(jnp.full((rows, n_dp), rank[s]) == 2, 0.0, weight)
        wl_all[s, y] = weight.astype(BF16)
        y_peers(
            lambda g, dev: copy_to(
                wl_all.at[s, y], wl_all.at[s, y], sent.at[5], al_r.at[s], dev
            ).start()
        )

    def shares(s, first, size):
        wait_bytes(wl_all.at[s, pl.ds(0, n_y - 1)], al_r.at[s])
        w_s = jnp.concatenate([wl_all[s, g].astype(F32) for g in range(n_y)], axis=0)
        for b in range(2):
            w_b = jnp.where(jnp.full((block, n_dp), owner[s]) == b, w_s, 0.0)
            w_full[b * block : (b + 1) * block, s * n_dp : (s + 1) * n_dp] = w_b.astype(BF16)
            w_full_t[s * n_dp : (s + 1) * n_dp, b * block : (b + 1) * block] = w_b.T.astype(BF16)
        for c in range(chunks // 2):
            share = mm(
                w_full_t[s * n_dp : (s + 1) * n_dp, :], q_ref[:, c * 256 : (c + 1) * 256]
            )
            to_messages(SCALE * share, first, n_dp, size, c)

    def send_slot(src, dst, ss, rs, own_sem):
        src[...] = wide[: n_dp * chunks, :].reshape(n_dp, chunks, 128).astype(BF16)
        for t in range(parts):
            part_peers(
                t,
                lambda i, there, dev: copy_to(src.at[i], dst.at[there], ss, rs, dev).start(),
            )
        pltpu.make_async_copy(src.at[my_place], dst.at[my_place], own_sem).start()

    listed_scores(0)
    log_a = log_total(0, (0, 1))
    listed_weights(0, (log_a,))
    shares(0, 0, chunks)
    wait_bytes(slab(recv1, 0).at[pl.ds(0, (n_dp - 1) * pair)], sent.at[1])
    wait_bytes(slab(recv1, 1).at[pl.ds(0, (n_dp - 1) * pair)], sent.at[2])
    send_slot(send2a, recv2a, sent.at[6], e2_r.at[0], loc.at[2])

    listed_scores(1)
    log_b = log_total(1, (1, 2, 3))
    for s in range(1, SLOTS):
        listed_weights(s, (log_a, log_b))
    shares(1, 0, chunks)
    send_slot(send2b, recv2b, sent.at[7], e2_r.at[1], loc.at[3])
    shares(2, 0, pair)
    shares(3, chunks, pair)
    send2c[...] = wide[: n_dp * pair, :].astype(BF16)
    for t in range(parts):
        part_peers(
            t,
            lambda i, there, dev: copy_to(
                at_row(send2c, i), at_row(recv2c, there), sent.at[8], e2c_r.at[t], dev
            ).start(),
        )
    pltpu.make_async_copy(at_row(send2c, my_place), at_row(recv2c, my_place), loc.at[4]).start()

    number_in = lax.broadcasted_iota(jnp.int32, (rows, p_ref.shape[0]), 1).astype(F32)
    ls_all[y] = jnp.zeros((8, 128), F32)
    for b in range(2):
        log_q = pick(early, log_a, log_b) if b == 0 else pick(early, log_b, log_a)
        sc = sum_in[b * rows : (b + 1) * rows, :]
        positive = number_in == own_cols[b][1]
        loss = log_q - jnp.sum(jnp.where(positive, sc, 0.0), axis=1, keepdims=True)
        weight = own_cols[b][0] * (jnp.exp(sc - log_q) - positive.astype(F32))
        wi_all[y, b * rows : (b + 1) * rows, :] = weight.astype(BF16)
        place = lax.broadcasted_iota(jnp.int32, (rows, 128), 1) - y * rows
        diag = place == lax.broadcasted_iota(jnp.int32, (rows, 128), 0)
        ls_all[y, b : b + 1, :] = jnp.sum(jnp.where(diag, loss, 0.0), axis=0, keepdims=True)
    y_peers(lambda g, dev: copy_to(wi_all.at[y], wi_all.at[y], sent.at[9], ai_r, dev).start())
    y_peers(lambda g, dev: copy_to(ls_all.at[y], ls_all.at[y], sent.at[10], ls_r, dev).start())
    wait_bytes(wi_all.at[pl.ds(0, n_y - 1)], ai_r)
    wait_bytes(ls_all.at[pl.ds(0, n_y - 1)], ls_r)
    loss_all = ls_all[0]
    for g in range(1, n_y):
        loss_all = loss_all + ls_all[g]
    loss_ref[...] = loss_all[0:2, :]
    for b in range(2):
        for g in range(n_y):
            w_in[b * block + g * rows : b * block + (g + 1) * rows, :] = wi_all[
                g, b * rows : (b + 1) * rows, :
            ]
    w_in_t = w_in[...].astype(F32).T.astype(BF16)
    for c in range(chunks // 2):
        cc = slice(c * 256, (c + 1) * 256)
        grad = mm(w_in[...], p_ref[:, cc]) + mm(w_full[...], listed[:, cc])
        gq_ref[:, cc] = (SCALE * grad).astype(BF16)
        own[:, cc] = SCALE * mm(w_in_t, q_ref[:, cc])

    for s, (src, own_sem) in enumerate(((recv2a, loc.at[2]), (recv2b, loc.at[3]))):
        wait_bytes(src.at[pl.ds(0, n_dp - 1)], e2_r.at[s])
        wait_bytes(src.at[my_place], own_sem)
        wide[: n_dp * chunks, :] = src[...].astype(F32).reshape(n_dp * chunks, 128)
        from_messages(shared, 0, n_dp, chunks, s * n_dp)
        for c in range(chunks // 2):
            cc = slice(c * 256, (c + 1) * 256)
            own[:, cc] += mm(
                hot_t[:, s * n_dp : (s + 1) * n_dp], shared[s * n_dp : (s + 1) * n_dp, cc]
            )
    for t in range(parts):
        wait_bytes(recv2c.at[pl.ds(t * peers * pair, part_sizes(t) * pair)], e2c_r.at[t])
        if t == my_part:
            wait_bytes(at_row(recv2c, my_place), loc.at[4])
        at = slice(t * peers * pair, (t + 1) * peers * pair)
        wide[at, :] = recv2c[at, :].astype(F32)
        for k in range(2):
            from_messages(
                shared, t * peers * pair + k * chunks, peers, pair, (2 + k) * n_dp + t * peers
            )
    for c in range(chunks // 2):
        cc = slice(c * 256, (c + 1) * 256)
        total = own[:, cc] + mm(hot_t[:, 2 * n_dp :], shared[2 * n_dp :, cc])
        gp_ref[:, cc] = total.astype(BF16)

    wait_bytes(ids.at[pl.ds(0, n_dp - 1)], sent.at[0])
    wait_bytes(recv_in.at[pl.ds(0, n_y - 1)], sent.at[3])
    wait_bytes(recv_l.at[:, pl.ds(0, n_y - 1)], sent.at[4])
    wait_bytes(wl_all.at[:, pl.ds(0, n_y - 1)], sent.at[5])
    wait_bytes(recv2a.at[pl.ds(0, n_dp - 1)], sent.at[6])
    wait_bytes(recv2b.at[pl.ds(0, n_dp - 1)], sent.at[7])
    wait_bytes(recv2c.at[pl.ds(0, (n_dp - 1) * pair)], sent.at[8])
    wait_bytes(wi_all.at[pl.ds(0, n_y - 1)], sent.at[9])
    wait_bytes(ls_all.at[pl.ds(0, n_y - 1)], sent.at[10])


def store(a, b, c, a_out, b_out, c_out, sems):
    copies = [
        pltpu.make_async_copy(src, dst, sems.at[k])
        for k, (src, dst) in enumerate(((a, a_out), (b, b_out), (c, c_out)))
    ]
    for copy in copies:
        copy.start()
    for copy in copies:
        copy.wait()


def per_device(z_count, queries, passages, block_lists, list_lengths, positive, loss_grad):
    n_dp, n_y = lax.axis_size("dp"), lax.axis_size("grp")
    n_blocks, shard_rows, width = passages.shape
    n_q = queries.shape[0]
    block = n_q // 2
    rows = block // n_y
    chunks = width // 128
    msg = SLOTS * chunks
    vmem = pl.BlockSpec(memory_space=pltpu.VMEM)
    hbm = pl.BlockSpec(memory_space=pltpu.HBM)
    parts = z_count // 4
    big = (n_dp * msg, 128)
    losses, gq, gp = pl.pallas_call(
        functools.partial(kernel, z_count),
        out_shape=(
            pltpu.VMEM((2, block), F32),
            pltpu.VMEM((n_q, width), BF16),
            pltpu.VMEM((n_blocks, width), BF16),
        ),
        in_specs=[hbm] * 6,
        out_specs=(vmem, vmem, vmem),
        scratch_shapes=[
            pltpu.VMEM((n_q, width), BF16),
            pltpu.VMEM((n_blocks, width), BF16),
            pltpu.SMEM(block_lists.shape, jnp.int32),
            pltpu.SMEM(list_lengths.shape, jnp.int32),
            pltpu.VMEM((2, block), jnp.int32),
            pltpu.VMEM((2, block), F32),
            pltpu.VMEM((n_dp, 1, 128), jnp.int32),
            pltpu.VMEM(big, BF16),
            pltpu.VMEM(big, BF16),
            pltpu.VMEM((n_dp, chunks, 128), BF16),
            pltpu.VMEM((n_dp, chunks, 128), BF16),
            pltpu.VMEM((n_dp, chunks, 128), BF16),
            pltpu.VMEM((n_dp, chunks, 128), BF16),
            pltpu.VMEM((n_dp * 2 * chunks, 128), BF16),
            pltpu.VMEM((n_dp * 2 * chunks, 128), BF16),
            pltpu.VMEM(big, F32),
            pltpu.VMEM((SLOTS * n_dp, width), BF16),
            pltpu.VMEM((SLOTS * n_dp, width), BF16),
            pltpu.VMEM((n_blocks, SLOTS * n_dp), BF16),
            pltpu.VMEM((n_y, 2 * rows, n_blocks), F32),
            pltpu.VMEM((n_y, 2 * rows, n_blocks), F32),
            pltpu.VMEM((2, n_y, 2, rows, n_dp), F32),
            pltpu.VMEM((2, n_y, 2, rows, n_dp), F32),
            pltpu.VMEM((2 * rows, n_blocks), F32),
            pltpu.VMEM((SLOTS, rows, n_dp), F32),
            pltpu.VMEM((2, n_q, 128), F32),
            pltpu.VMEM((SLOTS, n_y, rows, n_dp), BF16),
            pltpu.VMEM((n_y, 2 * rows, n_blocks), BF16),
            pltpu.VMEM((n_y, 8, 128), F32),
            pltpu.VMEM((n_q, n_blocks), BF16),
            pltpu.VMEM((n_q, SLOTS * n_dp), BF16),
            pltpu.VMEM((SLOTS * n_dp, n_q), BF16),
            pltpu.VMEM((n_blocks, width), F32),
            pltpu.SemaphoreType.DMA((6,)),
            pltpu.SemaphoreType.DMA((5,)),
            pltpu.SemaphoreType.DMA((11,)),
            pltpu.SemaphoreType.DMA((parts,)),
            pltpu.SemaphoreType.DMA((2,)),
            pltpu.SemaphoreType.DMA((2,)),
            pltpu.SemaphoreType.DMA((parts,)),
            pltpu.SemaphoreType.DMA,
            pltpu.SemaphoreType.DMA((2,)),
            pltpu.SemaphoreType.DMA((SLOTS,)),
            pltpu.SemaphoreType.DMA,
            pltpu.SemaphoreType.DMA,
        ],
        name="loss_and_gradients",
        compiler_params=pltpu.CompilerParams(
            collective_id=0, has_side_effects=True, vmem_limit_bytes=40 * 2**20
        ),
    )(
        *(
            pltpu.with_memory_space_constraint(x, pltpu.HBM)
            for x in (
                queries,
                passages.reshape(n_blocks * shard_rows, width),
                block_lists,
                list_lengths,
                positive.reshape(2, block),
                loss_grad.reshape(2, block),
            )
        )
    )
    losses, gq, gp = pl.pallas_call(
        store,
        out_shape=tuple(jax.ShapeDtypeStruct(x.shape, x.dtype) for x in (losses, gq, gp)),
        in_specs=[vmem] * 3,
        out_specs=(hbm,) * 3,
        scratch_shapes=[pltpu.SemaphoreType.DMA((3,))],
        name="store",
    )(*(pltpu.with_memory_space_constraint(x, pltpu.VMEM) for x in (losses, gq, gp)))
    return losses.reshape(n_q), gq, gp.reshape(passages.shape)


def solution(mesh):
    in_specs = (P("dp", "grp"), P(None, "dp", "grp"), P("dp", None), P("dp"), P("dp"), P("dp"))
    out_specs = (P("dp"), P("dp", "grp"), P(None, "dp", "grp"))
    z_count = mesh.shape["dp"] // 8
    return jax.shard_map(
        functools.partial(per_device, z_count),
        mesh=mesh, in_specs=in_specs, out_specs=out_specs, check_vma=False,
    )
```

```python
import functools
import math

import jax
import jax.numpy as jnp
from jax import lax
from jax.experimental import pallas as pl
from jax.experimental.pallas import tpu as pltpu
from jax.sharding import PartitionSpec as P

D = 4096
SCALE = 3.0 / math.sqrt(D)
SLOTS = 4
LOGICAL = pl.DeviceIdType.LOGICAL
NN = (((1,), (0,)), ((), ()))
NT = (((1,), (1,)), ((), ()))
F32, BF16 = jnp.float32, jnp.bfloat16


def mm(a, b, dims=NN):
    return lax.dot_general(a, b, dims, preferred_element_type=F32)


def kernel(
    z_count,
    q_hbm, p_hbm, lists_hbm, lens_hbm, pos_hbm, lg_hbm,
    loss_ref, gq_ref, gp_ref,
    q_ref, p_ref, lists_ref, lens_ref, pos_ref, lg_ref,
    ids, send1, recv1, send2a, recv2a, send2b, recv2b, send2c, recv2c, wide, listed, shared, hot_t,
    part_in, recv_in, part_l, recv_l, sum_in, sum_l, cols,
    wl_all, wi_all, ls_all, w_in, w_full, w_full_t, own,
    in_s, loc, sent, ids_r, e1_r, e2_r, e2c_r, ri_r, rl_r, al_r, ai_r, ls_r,
):
    me = lax.axis_index("dp")
    y = lax.axis_index("grp")
    n_dp = lax.axis_size("dp")
    n_y = lax.axis_size("grp")
    plane = n_dp // z_count
    my_z, my_xc = me // plane, me % plane
    block = q_ref.shape[0] // 2
    rows = block // n_y
    chunks = q_ref.shape[1] // 128
    pair = 2 * chunks
    far = z_count // 2
    order = [far, far - 1, 1 - far, 0]
    for h in range(far - 2, 0, -1):
        order += [h, -h]
    opposite = [order.index(-dz) if -dz in order else order.index(dz) for dz in order]
    parts = z_count // 4
    peers = 4 * plane
    zs = [lax.rem(my_z + dz + z_count, z_count) for dz in order]
    base = [z * (plane * n_y) + y for z in zs]
    my_part = order.index(0) // 4
    my_place = order.index(0) * plane + my_xc
    first_out = [2, 0, 1, 3] if parts == 4 else list(range(parts))

    def copy_to(src, dst, ss, rs, dev):
        return pltpu.make_async_remote_copy(
            src_ref=src, dst_ref=dst, send_sem=ss, recv_sem=rs, device_id=dev, device_id_type=LOGICAL
        )

    def wait_bytes(ref, sem):
        pltpu.make_async_copy(ref, ref, sem).wait()

    def y_peers(body):
        for k in range(1, n_y):
            g = lax.rem(y + k, n_y)
            body(g, me * n_y + g)

    def part_peers(t, body):
        def step(k, carry):
            xc = lax.rem(my_xc + k, plane)
            for i in range(4 * t, 4 * t + 4):
                body(i * plane + xc, opposite[i] * plane + my_xc, base[i] + xc * n_y)
            return carry

        lax.fori_loop(1, plane, step, 0)
        for i in range(4 * t, 4 * t + 4):
            if order[i] != 0:
                body(i * plane + my_xc, opposite[i] * plane + my_xc, base[i] + my_xc * n_y)

    def part_sizes(t):
        return peers - 1 if t == my_part else peers

    copies_in = [
        pltpu.make_async_copy(src, dst, in_s.at[k])
        for k, (src, dst) in enumerate(
            (
                (lists_hbm, lists_ref), (lens_hbm, lens_ref), (q_hbm, q_ref),
                (p_hbm, p_ref), (pos_hbm, pos_ref), (lg_hbm, lg_ref),
            )
        )
    ]
    for c in copies_in:
        c.start()

    barrier = pltpu.get_barrier_semaphore()

    def greet(dev):
        pl.semaphore_signal(barrier, inc=1, device_id=dev, device_id_type=LOGICAL)

    for i, dz in enumerate(order):
        if dz != 0:
            for xc in range(plane):
                greet(base[i] + xc * n_y)
    for k in range(1, plane):
        greet(base[order.index(0)] + lax.rem(my_xc + k, plane) * n_y)
    y_peers(lambda g, dev: greet(dev))

    copies_in[0].wait()
    copies_in[1].wait()
    len0, len1 = lens_ref[0], lens_ref[1]
    swap = len1 < len0
    early = jnp.where(swap, 1, 0)
    len_a, len_b = jnp.where(swap, len1, len0), jnp.where(swap, len0, len1)
    list_a = [jnp.where(swap, lists_ref[1, k], lists_ref[0, k]) for k in range(3)]
    list_b = [jnp.where(swap, lists_ref[0, k], lists_ref[1, k]) for k in range(3)]
    lane = lax.broadcasted_iota(jnp.int32, (1, 128), 1)
    id_row = jnp.full((1, 128), -1, jnp.int32)
    rank = []
    for s in range(SLOTS):
        k = s - len_a
        id_b = jnp.where(k == 0, list_b[0], jnp.where(k == 1, list_b[1], list_b[2]))
        in_a = jnp.int32(s) < len_a
        in_b = k < len_b
        slot_id = jnp.where(in_a, list_a[min(s, 2)], jnp.where(in_b, id_b, -1))
        rank.append(jnp.where(in_a, 0, jnp.where(in_b, 1, 2)))
        id_row = jnp.where(lane == s, slot_id, id_row)
    owner = [jnp.where(r == 0, early, jnp.where(r == 1, 1 - early, 2)) for r in rank]
    ids[my_place] = id_row

    for c in copies_in[2:]:
        c.wait()
    scores = mm(q_ref[...], p_ref[...], NT)
    for g in range(n_y):
        for b in range(2):
            part_in[g, b * rows : (b + 1) * rows, :] = scores[
                b * block + g * rows : b * block + (g + 1) * rows
            ]

    pl.semaphore_wait(barrier, n_dp - 1 + n_y - 1)

    for t in first_out:
        part_peers(
            t,
            lambda i, there, dev: copy_to(
                ids.at[my_place], ids.at[there], sent.at[0], ids_r.at[t], dev
            ).start(),
        )

    def to_messages(value, first, n, size, c):
        for h in range(2):
            wide[pl.ds(first + 2 * c + h, n, stride=size), :] = value[:, h * 128 : (h + 1) * 128]

    def from_messages(dst, first, n, size, row):
        for c in range(chunks):
            dst[row : row + n, c * 128 : (c + 1) * 128] = wide[
                pl.ds(first + c, n, stride=size), :
            ].astype(BF16)

    def at_row(ref, p):
        return ref.at[pl.ds(pl.multiple_of(p * pair, pair), pair)]

    def slab(ref, h):
        return ref.at[pl.ds(h * n_dp * pair, n_dp * pair)]

    number = lax.broadcasted_iota(jnp.int32, (peers, p_ref.shape[0]), 1)
    for h in range(2):
        src, dst = slab(send1, h), slab(recv1, h)
        for t in first_out:
            if h == 0:
                wait_bytes(ids.at[pl.ds(t * peers, part_sizes(t))], ids_r.at[t])
            id_mat = ids[t * peers : (t + 1) * peers].reshape(peers, 128)
            hot = jnp.concatenate(
                [(id_mat[:, s : s + 1] == number).astype(F32) for s in (2 * h, 2 * h + 1)], axis=0
            ).astype(BF16)
            first = (h * n_dp + t * peers) * pair
            for c in range(chunks // 2):
                value = mm(hot, p_ref[:, c * 256 : (c + 1) * 256])
                for k in range(2):
                    to_messages(value[k * peers : (k + 1) * peers], first + k * chunks, peers, pair, c)
            at = slice(first, first + peers * pair)
            send1[at, :] = wide[at, :].astype(BF16)
            part_peers(
                t,
                lambda i, there, dev: copy_to(
                    at_row(src, i), at_row(dst, there), sent.at[1 + h], e1_r.at[h], dev
                ).start(),
            )
        pltpu.make_async_copy(at_row(src, my_place), at_row(dst, my_place), loc.at[h]).start()

    y_peers(lambda g, dev: copy_to(part_in.at[g], recv_in.at[y], sent.at[3], ri_r, dev).start())
    for b in range(2):
        cols[0, b * block : (b + 1) * block, :] = jnp.broadcast_to(
            lg_ref[b : b + 1, :], (block, 128)
        ).T
        column = (pos_ref[b : b + 1, :] // block).astype(F32)
        cols[1, b * block : (b + 1) * block, :] = jnp.broadcast_to(column, (block, 128)).T
    id_mat = ids[...].reshape(n_dp, 128)
    number = lax.broadcasted_iota(jnp.int32, (n_dp, p_ref.shape[0]), 1)
    for s in range(SLOTS):
        hot_t[:, s * n_dp : (s + 1) * n_dp] = (id_mat[:, s : s + 1] == number).astype(F32).T.astype(BF16)
    recv_in[y] = part_in[y]
    wait_bytes(recv_in.at[pl.ds(0, n_y - 1)], ri_r)
    total = recv_in[0]
    for g in range(1, n_y):
        total = total + recv_in[g]
    sum_in[...] = SCALE * total
    own_cols = []
    for b in range(2):
        at = pl.ds(pl.multiple_of(b * block + y * rows, rows), rows)
        own_cols.append((cols[0, at, :][:, :1], cols[1, at, :][:, :1]))

    def listed_scores(h):
        got = slab(recv1, h)
        wait_bytes(got.at[pl.ds(0, (n_dp - 1) * pair)], e1_r.at[h])
        wait_bytes(at_row(got, my_place), loc.at[h])
        at = slice(h * n_dp * pair, (h + 1) * n_dp * pair)
        wide[at, :] = recv1[at, :].astype(F32)
        for k in range(2):
            from_messages(listed, h * n_dp * pair + k * chunks, n_dp, pair, (2 * h + k) * n_dp)
        scores = mm(q_ref[...], listed[2 * h * n_dp : 2 * (h + 1) * n_dp, :], NT)
        for k in range(2):
            of_1 = jnp.full((block, n_dp), owner[2 * h + k]) == 1
            cc = slice(k * n_dp, (k + 1) * n_dp)
            mine = jnp.where(of_1, scores[block:, cc], scores[:block, cc])
            for g in range(n_y):
                part_l[h, g, k] = mine[g * rows : (g + 1) * rows]
        y_peers(
            lambda g, dev: copy_to(
                part_l.at[h, g], recv_l.at[h, y], sent.at[4], rl_r.at[h], dev
            ).start()
        )
        recv_l[h, y] = part_l[h, y]
        wait_bytes(recv_l.at[h, pl.ds(0, n_y - 1)], rl_r.at[h])
        for k in range(2):
            total = recv_l[h, 0, k]
            for g in range(1, n_y):
                total = total + recv_l[h, g, k]
            sum_l[2 * h + k] = SCALE * total

    def pick(which, a, b):
        return jnp.where(jnp.full(a.shape, which) == 1, b, a)

    def log_total(r, slots):
        blk = early if r == 0 else 1 - early
        sc = pick(blk, sum_in[:rows, :], sum_in[rows:, :])
        opened = [
            jnp.where(jnp.full((rows, n_dp), rank[s]) == r, sum_l[s], -jnp.inf) for s in slots
        ]
        best = opened[0]
        for o in opened[1:]:
            best = jnp.maximum(best, o)
        top = jnp.maximum(
            jnp.max(sc, axis=1, keepdims=True), jnp.max(best, axis=1, keepdims=True)
        )
        terms = jnp.exp(opened[0] - top)
        for o in opened[1:]:
            terms = terms + jnp.exp(o - top)
        acc = jnp.sum(jnp.exp(sc - top), axis=1, keepdims=True) + jnp.sum(
            terms, axis=1, keepdims=True
        )
        return top + jnp.log(acc)

    grads = [
        pick(early, own_cols[0][0], own_cols[1][0]),
        pick(1 - early, own_cols[0][0], own_cols[1][0]),
    ]

    def listed_weights(s, logs):
        log_s = pick(rank[s], logs[0], logs[-1])
        grad_s = pick(rank[s], grads[0], grads[1])
        weight = grad_s * jnp.exp(sum_l[s] - log_s)
        weight = jnp.where(jnp.full((rows, n_dp), rank[s]) == 2, 0.0, weight)
        wl_all[s, y] = weight.astype(BF16)
        y_peers(
            lambda g, dev: copy_to(
                wl_all.at[s, y], wl_all.at[s, y], sent.at[5], al_r.at[s], dev
            ).start()
        )

    def shares(s, first, size):
        wait_bytes(wl_all.at[s, pl.ds(0, n_y - 1)], al_r.at[s])
        w_s = jnp.concatenate([wl_all[s, g].astype(F32) for g in range(n_y)], axis=0)
        for b in range(2):
            w_b = jnp.where(jnp.full((block, n_dp), owner[s]) == b, w_s, 0.0)
            w_full[b * block : (b + 1) * block, s * n_dp : (s + 1) * n_dp] = w_b.astype(BF16)
            w_full_t[s * n_dp : (s + 1) * n_dp, b * block : (b + 1) * block] = w_b.T.astype(BF16)
        for c in range(chunks // 2):
            share = mm(
                w_full_t[s * n_dp : (s + 1) * n_dp, :], q_ref[:, c * 256 : (c + 1) * 256]
            )
            to_messages(SCALE * share, first, n_dp, size, c)

    def send_slot(src, dst, ss, rs, own_sem):
        src[...] = wide[: n_dp * chunks, :].reshape(n_dp, chunks, 128).astype(BF16)
        for t in range(parts):
            part_peers(
                t,
                lambda i, there, dev: copy_to(src.at[i], dst.at[there], ss, rs, dev).start(),
            )
        pltpu.make_async_copy(src.at[my_place], dst.at[my_place], own_sem).start()

    listed_scores(0)
    log_a = log_total(0, (0, 1))
    listed_weights(0, (log_a,))
    shares(0, 0, chunks)
    wait_bytes(slab(recv1, 0).at[pl.ds(0, (n_dp - 1) * pair)], sent.at[1])
    wait_bytes(slab(recv1, 1).at[pl.ds(0, (n_dp - 1) * pair)], sent.at[2])
    send_slot(send2a, recv2a, sent.at[6], e2_r.at[0], loc.at[2])

    listed_scores(1)
    log_b = log_total(1, (1, 2, 3))
    for s in range(1, SLOTS):
        listed_weights(s, (log_a, log_b))
    shares(1, 0, chunks)
    send_slot(send2b, recv2b, sent.at[7], e2_r.at[1], loc.at[3])
    shares(2, 0, pair)
    shares(3, chunks, pair)
    send2c[...] = wide[: n_dp * pair, :].astype(BF16)
    for t in range(parts):
        part_peers(
            t,
            lambda i, there, dev: copy_to(
                at_row(send2c, i), at_row(recv2c, there), sent.at[8], e2c_r.at[t], dev
            ).start(),
        )
    pltpu.make_async_copy(at_row(send2c, my_place), at_row(recv2c, my_place), loc.at[4]).start()

    number_in = lax.broadcasted_iota(jnp.int32, (rows, p_ref.shape[0]), 1).astype(F32)
    ls_all[y] = jnp.zeros((8, 128), F32)
    for b in range(2):
        log_q = pick(early, log_a, log_b) if b == 0 else pick(early, log_b, log_a)
        sc = sum_in[b * rows : (b + 1) * rows, :]
        positive = number_in == own_cols[b][1]
        loss = log_q - jnp.sum(jnp.where(positive, sc, 0.0), axis=1, keepdims=True)
        weight = own_cols[b][0] * (jnp.exp(sc - log_q) - positive.astype(F32))
        wi_all[y, b * rows : (b + 1) * rows, :] = weight.astype(BF16)
        place = lax.broadcasted_iota(jnp.int32, (rows, 128), 1) - y * rows
        diag = place == lax.broadcasted_iota(jnp.int32, (rows, 128), 0)
        ls_all[y, b : b + 1, :] = jnp.sum(jnp.where(diag, loss, 0.0), axis=0, keepdims=True)
    y_peers(lambda g, dev: copy_to(wi_all.at[y], wi_all.at[y], sent.at[9], ai_r, dev).start())
    y_peers(lambda g, dev: copy_to(ls_all.at[y], ls_all.at[y], sent.at[10], ls_r, dev).start())
    wait_bytes(wi_all.at[pl.ds(0, n_y - 1)], ai_r)
    wait_bytes(ls_all.at[pl.ds(0, n_y - 1)], ls_r)
    loss_all = ls_all[0]
    for g in range(1, n_y):
        loss_all = loss_all + ls_all[g]
    loss_ref[...] = loss_all[0:2, :]
    for b in range(2):
        for g in range(n_y):
            w_in[b * block + g * rows : b * block + (g + 1) * rows, :] = wi_all[
                g, b * rows : (b + 1) * rows, :
            ]
    w_in_t = w_in[...].astype(F32).T.astype(BF16)
    for c in range(chunks // 2):
        cc = slice(c * 256, (c + 1) * 256)
        grad = mm(w_in[...], p_ref[:, cc]) + mm(w_full[...], listed[:, cc])
        gq_ref[:, cc] = (SCALE * grad).astype(BF16)
        own[:, cc] = SCALE * mm(w_in_t, q_ref[:, cc])

    for s, (src, own_sem) in enumerate(((recv2a, loc.at[2]), (recv2b, loc.at[3]))):
        wait_bytes(src.at[pl.ds(0, n_dp - 1)], e2_r.at[s])
        wait_bytes(src.at[my_place], own_sem)
        wide[: n_dp * chunks, :] = src[...].astype(F32).reshape(n_dp * chunks, 128)
        from_messages(shared, 0, n_dp, chunks, s * n_dp)
        for c in range(chunks // 2):
            cc = slice(c * 256, (c + 1) * 256)
            own[:, cc] += mm(
                hot_t[:, s * n_dp : (s + 1) * n_dp], shared[s * n_dp : (s + 1) * n_dp, cc]
            )
    for t in range(parts):
        wait_bytes(recv2c.at[pl.ds(t * peers * pair, part_sizes(t) * pair)], e2c_r.at[t])
        if t == my_part:
            wait_bytes(at_row(recv2c, my_place), loc.at[4])
        at = slice(t * peers * pair, (t + 1) * peers * pair)
        wide[at, :] = recv2c[at, :].astype(F32)
        for k in range(2):
            from_messages(
                shared, t * peers * pair + k * chunks, peers, pair, (2 + k) * n_dp + t * peers
            )
    for c in range(chunks // 2):
        cc = slice(c * 256, (c + 1) * 256)
        total = own[:, cc] + mm(hot_t[:, 2 * n_dp :], shared[2 * n_dp :, cc])
        gp_ref[:, cc] = total.astype(BF16)

    wait_bytes(ids.at[pl.ds(0, n_dp - 1)], sent.at[0])
    wait_bytes(recv_in.at[pl.ds(0, n_y - 1)], sent.at[3])
    wait_bytes(recv_l.at[:, pl.ds(0, n_y - 1)], sent.at[4])
    wait_bytes(wl_all.at[:, pl.ds(0, n_y - 1)], sent.at[5])
    wait_bytes(recv2a.at[pl.ds(0, n_dp - 1)], sent.at[6])
    wait_bytes(recv2b.at[pl.ds(0, n_dp - 1)], sent.at[7])
    wait_bytes(recv2c.at[pl.ds(0, (n_dp - 1) * pair)], sent.at[8])
    wait_bytes(wi_all.at[pl.ds(0, n_y - 1)], sent.at[9])
    wait_bytes(ls_all.at[pl.ds(0, n_y - 1)], sent.at[10])


def store(a, b, c, a_out, b_out, c_out, sems):
    copies = [
        pltpu.make_async_copy(src, dst, sems.at[k])
        for k, (src, dst) in enumerate(((a, a_out), (b, b_out), (c, c_out)))
    ]
    for copy in copies:
        copy.start()
    for copy in copies:
        copy.wait()


def per_device(z_count, queries, passages, block_lists, list_lengths, positive, loss_grad):
    n_dp, n_y = lax.axis_size("dp"), lax.axis_size("grp")
    n_blocks, shard_rows, width = passages.shape
    n_q = queries.shape[0]
    block = n_q // 2
    rows = block // n_y
    chunks = width // 128
    msg = SLOTS * chunks
    vmem = pl.BlockSpec(memory_space=pltpu.VMEM)
    hbm = pl.BlockSpec(memory_space=pltpu.HBM)
    parts = z_count // 4
    big = (n_dp * msg, 128)
    losses, gq, gp = pl.pallas_call(
        functools.partial(kernel, z_count),
        out_shape=(
            pltpu.VMEM((2, block), F32),
            pltpu.VMEM((n_q, width), BF16),
            pltpu.VMEM((n_blocks, width), BF16),
        ),
        in_specs=[hbm] * 6,
        out_specs=(vmem, vmem, vmem),
        scratch_shapes=[
            pltpu.VMEM((n_q, width), BF16),
            pltpu.VMEM((n_blocks, width), BF16),
            pltpu.SMEM(block_lists.shape, jnp.int32),
            pltpu.SMEM(list_lengths.shape, jnp.int32),
            pltpu.VMEM((2, block), jnp.int32),
            pltpu.VMEM((2, block), F32),
            pltpu.VMEM((n_dp, 1, 128), jnp.int32),
            pltpu.VMEM(big, BF16),
            pltpu.VMEM(big, BF16),
            pltpu.VMEM((n_dp, chunks, 128), BF16),
            pltpu.VMEM((n_dp, chunks, 128), BF16),
            pltpu.VMEM((n_dp, chunks, 128), BF16),
            pltpu.VMEM((n_dp, chunks, 128), BF16),
            pltpu.VMEM((n_dp * 2 * chunks, 128), BF16),
            pltpu.VMEM((n_dp * 2 * chunks, 128), BF16),
            pltpu.VMEM(big, F32),
            pltpu.VMEM((SLOTS * n_dp, width), BF16),
            pltpu.VMEM((SLOTS * n_dp, width), BF16),
            pltpu.VMEM((n_blocks, SLOTS * n_dp), BF16),
            pltpu.VMEM((n_y, 2 * rows, n_blocks), F32),
            pltpu.VMEM((n_y, 2 * rows, n_blocks), F32),
            pltpu.VMEM((2, n_y, 2, rows, n_dp), F32),
            pltpu.VMEM((2, n_y, 2, rows, n_dp), F32),
            pltpu.VMEM((2 * rows, n_blocks), F32),
            pltpu.VMEM((SLOTS, rows, n_dp), F32),
            pltpu.VMEM((2, n_q, 128), F32),
            pltpu.VMEM((SLOTS, n_y, rows, n_dp), BF16),
            pltpu.VMEM((n_y, 2 * rows, n_blocks), BF16),
            pltpu.VMEM((n_y, 8, 128), F32),
            pltpu.VMEM((n_q, n_blocks), BF16),
            pltpu.VMEM((n_q, SLOTS * n_dp), BF16),
            pltpu.VMEM((SLOTS * n_dp, n_q), BF16),
            pltpu.VMEM((n_blocks, width), F32),
            pltpu.SemaphoreType.DMA((6,)),
            pltpu.SemaphoreType.DMA((5,)),
            pltpu.SemaphoreType.DMA((11,)),
            pltpu.SemaphoreType.DMA((parts,)),
            pltpu.SemaphoreType.DMA((2,)),
            pltpu.SemaphoreType.DMA((2,)),
            pltpu.SemaphoreType.DMA((parts,)),
            pltpu.SemaphoreType.DMA,
            pltpu.SemaphoreType.DMA((2,)),
            pltpu.SemaphoreType.DMA((SLOTS,)),
            pltpu.SemaphoreType.DMA,
            pltpu.SemaphoreType.DMA,
        ],
        name="loss_and_gradients",
        compiler_params=pltpu.CompilerParams(
            collective_id=0, has_side_effects=True, vmem_limit_bytes=40 * 2**20
        ),
    )(
        *(
            pltpu.with_memory_space_constraint(x, pltpu.HBM)
            for x in (
                queries,
                passages.reshape(n_blocks * shard_rows, width),
                block_lists,
                list_lengths,
                positive.reshape(2, block),
                loss_grad.reshape(2, block),
            )
        )
    )
    losses, gq, gp = pl.pallas_call(
        store,
        out_shape=tuple(jax.ShapeDtypeStruct(x.shape, x.dtype) for x in (losses, gq, gp)),
        in_specs=[vmem] * 3,
        out_specs=(hbm,) * 3,
        scratch_shapes=[pltpu.SemaphoreType.DMA((3,))],
        name="store",
    )(*(pltpu.with_memory_space_constraint(x, pltpu.VMEM) for x in (losses, gq, gp)))
    return losses.reshape(n_q), gq, gp.reshape(passages.shape)


def solution(mesh):
    in_specs = (P("dp", "grp"), P(None, "dp", "grp"), P("dp", None), P("dp"), P("dp"), P("dp"))
    out_specs = (P("dp"), P("dp", "grp"), P(None, "dp", "grp"))
    z_count = mesh.shape["dp"] // 8
    return jax.shard_map(
        functools.partial(per_device, z_count),
        mesh=mesh, in_specs=in_specs, out_specs=out_specs, check_vma=False,
    )
```
